32 devices in a mesh: src: 4 (over y, x), rcv: 8 (over z, core).
Axes of the slice: x: 2, y: 2, z: 4, core: 2. Of those that a mesh axis runs over, the one named last changes fastest.
Arguments:
- traces: float32 [512, 512, 1024], P('src', 'rcv'), may hold values from -6 to 6
- freq_index: int32 [256], replicated, may hold values from 1 to 511, as said below
- primaries: float32 [256, 2, 512, 512], P(('src', 'rcv')), may hold values from -0.1875 to 0.1875
Outputs:
- residual: float32 [256, 2, 512, 512], P(('src', 'rcv'))
- residual_next: float32 [256, 2, 512, 512], P(('src', 'rcv'))
The draws below stay inside these ranges and needn't reach their ends.
Inputs may be any that keep to these rules, and one draw needn't show every extreme that they name: `freq_index`: sorted ascending; repeats possible; the first is 1 and the last is 511.
All inputs are finite; a program needn't handle non-finite values.
Results may differ from the reference program's by a relative error of at most 0.00012.
Values sent between devices are 32-bit elements; how exact they have to be, the bound alone decides.
No kernel may reach another device: no remote copies, remote signals or barrier semaphores. Data moves between devices by JAX's collectives and lax.ppermute only.
A program may use at most 256 MiB of HBM per device.

```python
import math
import jax
import jax.numpy as jnp
from jax import lax

NS = 512
NR = 512
NT = 1024
NF = 256
N_SRC = 4


def draw_freq_index(key, part):
    values = jax.random.randint(jax.random.fold_in(key, 17), (NF,), 1, NT // 2)
    values = values.at[0].set(1).at[NF - 1].set(NT // 2 - 1)
    return jnp.sort(values).astype(jnp.int32)


def levels(own_key, extent, split, low, top_value):
    loudness = 1.0
    for position, blocks in split:
        draws = jax.random.uniform(jax.random.fold_in(jax.random.fold_in(own_key, 6), position), (blocks,), jnp.float32, low / len(split), top_value / len(split))
        loudness = loudness * jnp.repeat(jnp.exp(draws), extent[position] // blocks).reshape((-1,) + (1,) * (len(extent) - 1 - position))
    return loudness


def gaussian(own_key, shape, spread, most, pieces=(), kind=jnp.bfloat16):
    entries = jax.random.normal(own_key, shape, jnp.float32) * spread
    if len(pieces) > 0:
        entries = levels(own_key, shape, pieces, -0.22, 0.18) * entries
    return jnp.clip(entries, min=-most, max=most).astype(kind)


def setup_inputs(seed: int = 0) -> dict:
    key_of = jax.random.split(jax.random.key(seed), 4)
    traces = gaussian(key_of[0], (NS, NR, NT), 1.0, 6.0, ((0, 4), (1, 8)), jnp.float32)
    freq_index = draw_freq_index(jax.random.fold_in(key_of[3], 71), 0)
    primaries = gaussian(key_of[2], (NF, 2, NS, NR), (2 * NS) ** -0.5, 0.1875, ((0, 32),), jnp.float32)
    return dict(traces=traces, freq_index=freq_index, primaries=primaries)


def freq_table(freq_index, samples):
    times = jnp.arange(samples, dtype=jnp.int32)
    phase = freq_index[:, None] * times[None, :] % samples
    angle = phase.astype(jnp.float32) * (2.0 * math.pi / samples)
    return jnp.stack([jnp.cos(angle), -jnp.sin(angle)], axis=1) / math.sqrt(samples)

def matrix_product(left, right):
    return jnp.einsum('fij,fjk->fik', left, right, precision=lax.Precision.HIGHEST)

def complex_product(left_re, left_im, right_re, right_im, adjoint):
    if adjoint:
        right_re = jnp.swapaxes(right_re, 1, 2)
        right_im = -jnp.swapaxes(right_im, 1, 2)
    real_part = matrix_product(left_re, right_re) - matrix_product(left_im, right_im)
    imag_part = matrix_product(left_re, right_im) + matrix_product(left_im, right_re)
    return (real_part, imag_part)

def solve_step(spectrum, primaries, weights):
    data_re = 0.5 * (spectrum[:, 0] + jnp.swapaxes(spectrum[:, 0], 1, 2))
    data_im = 0.5 * (spectrum[:, 1] + jnp.swapaxes(spectrum[:, 1], 1, 2))
    model_re, model_im = complex_product(primaries[:, 0], primaries[:, 1], data_re, data_im, False)
    resid_re = data_re - model_re
    resid_im = data_im - model_im
    grad_re, grad_im = complex_product(resid_re, resid_im, data_re, data_im, True)
    pred_re, pred_im = complex_product(grad_re, grad_im, data_re, data_im, False)
    scaled = weights[:, None, None]
    numer = jnp.sum(scaled * (resid_re * pred_re + resid_im * pred_im))
    denom = jnp.sum(scaled * (pred_re * pred_re + pred_im * pred_im))
    return (jnp.stack([resid_re, resid_im], 1), jnp.stack([pred_re, pred_im], 1), numer, denom)

def reference(traces, freq_index, primaries):
    table = freq_table(freq_index, NT)
    blocks = traces.reshape(N_SRC, NS // N_SRC, NR, NT)

    def transform(block):
        return jnp.einsum('kct,srt->kcsr', table, block, precision=lax.Precision.HIGHEST)
    spectrum = lax.map(transform, blocks)
    spectrum = jnp.transpose(spectrum, (1, 2, 0, 3, 4)).reshape(NF, 2, NS, NR)
    weights = freq_index.astype(jnp.float32) / (NT // 2)

    def per_freq(items):
        return solve_step(items[0], items[1], items[2])
    resid, pred, numer, denom = lax.map(per_freq, (spectrum[:, None], primaries[:, None], weights[:, None]))
    resid = resid.reshape(NF, 2, NS, NR)
    pred = pred.reshape(NF, 2, NS, NR)
    step_size = jnp.sum(numer) / jnp.sum(denom)
    return (resid, resid - step_size * pred)
```

```python
import functools
import math

import jax
import jax.numpy as jnp
from jax import lax
from jax.experimental import pallas as pl
from jax.experimental.pallas import tpu as pltpu
from jax.sharding import PartitionSpec as P

AXES = ("src", "rcv")
LANES = 128
COST_SCALE = 100
STREAMS = 4
STREAM_ROWS = 4
VMEM_BYTES = 56 * 1024 * 1024
UPDATE_VMEM_BYTES = 14 * 1024 * 1024
F32 = jnp.float32
BF16 = jnp.bfloat16


def freq_table(freq_index, samples):
    times = jnp.arange(samples, dtype=jnp.int32)
    phase = freq_index[:, None] * times[None, :] % samples
    angle = phase.astype(jnp.float32) * (2.0 * math.pi / samples)
    return jnp.stack([jnp.cos(angle), -jnp.sin(angle)], axis=1) / math.sqrt(samples)


def matrix_product(left, right):
    return jnp.einsum("fij,fjk->fik", left, right, precision=lax.Precision.HIGHEST)


def complex_product(left_re, left_im, right_re, right_im, adjoint):
    if adjoint:
        right_re = jnp.swapaxes(right_re, 1, 2)
        right_im = -jnp.swapaxes(right_im, 1, 2)
    real_part = matrix_product(left_re, right_re) - matrix_product(left_im, right_im)
    imag_part = matrix_product(left_re, right_im) + matrix_product(left_im, right_re)
    return (real_part, imag_part)


def plain_step(traces, freq_index, primaries):
    src_local, rcv_local, samples = traces.shape
    n_src = lax.axis_size("src")
    n_rcv = lax.axis_size("rcv")
    table = freq_table(freq_index, samples)
    flat = traces.reshape(src_local * rcv_local, samples)
    spectrum = lax.dot_general(
        table,
        flat,
        (((2,), (1,)), ((), ())),
        precision=lax.Precision.HIGHEST,
        preferred_element_type=jnp.float32,
    )
    spectrum = spectrum[None]
    freq_local = primaries.shape[0]
    arrived = lax.all_to_all(spectrum, AXES, split_axis=1, concat_axis=0, tiled=True)
    arrived = arrived.reshape(n_src, n_rcv, freq_local, 2, src_local, rcv_local)
    arrived = jnp.transpose(arrived, (2, 3, 0, 4, 1, 5))
    whole = arrived.reshape(freq_local, 2, n_src * src_local, n_rcv * rcv_local)
    data_re = 0.5 * (whole[:, 0] + jnp.swapaxes(whole[:, 0], 1, 2))
    data_im = 0.5 * (whole[:, 1] + jnp.swapaxes(whole[:, 1], 1, 2))
    model_re, model_im = complex_product(primaries[:, 0], primaries[:, 1], data_re, data_im, False)
    resid_re = data_re - model_re
    resid_im = data_im - model_im
    grad_re, grad_im = complex_product(resid_re, resid_im, data_re, data_im, True)
    pred_re, pred_im = complex_product(grad_re, grad_im, data_re, data_im, False)
    offset = (lax.axis_index("src") * n_rcv + lax.axis_index("rcv")) * freq_local
    weights = freq_index.astype(jnp.float32) / (samples // 2)
    weights = lax.dynamic_slice_in_dim(weights, offset, freq_local)
    scaled = weights[:, None, None]
    numer = jnp.sum(scaled * (resid_re * pred_re + resid_im * pred_im))
    denom = jnp.sum(scaled * (pred_re * pred_re + pred_im * pred_im))
    numer, denom = lax.psum((numer, denom), AXES)
    step_size = numer / denom
    resid = jnp.stack([resid_re, resid_im], 1)
    pred = jnp.stack([pred_re, pred_im], 1)
    return (resid, resid - step_size * pred)


def params(**more):
    return pltpu.CompilerParams(vmem_limit_bytes=VMEM_BYTES, **more)


def cost(flops, moved):
    return pl.CostEstimate(flops=int(flops) // COST_SCALE, bytes_accessed=int(moved) // COST_SCALE, transcendentals=0)


def halves(x):
    high = x.astype(BF16)
    return high, (x - high.astype(F32)).astype(BF16)


def product(left, right):
    dot = functools.partial(jnp.dot, preferred_element_type=F32)
    return dot(left[0], right[0]) + (dot(left[0], right[1]) + dot(left[1], right[0]))


def transform_kernel(splits, streams, table_ref, *refs):
    traces_refs, out_refs = refs[:streams], refs[streams:][-len(splits) :]
    rows, width, samples = traces_refs[0].shape
    count = table_ref.shape[0] // 4
    is_left = lax.broadcasted_iota(jnp.int32, (1, LANES), 1) < width
    contract = (((1,), (1,)), ((), ()))
    for stream, traces_ref in enumerate(traces_refs):
        x = traces_ref[...].reshape(rows * width, samples)
        high, low = halves(x)
        first = lax.dot_general(table_ref[...], high, contract, preferred_element_type=F32)
        second = lax.dot_general(table_ref[: 2 * count], low, contract, preferred_element_type=F32)
        spectrum = first[: 2 * count] + first[2 * count :] + second
        for pair in range(rows // 2):
            cols = slice(pair * LANES, (pair + 1) * LANES)
            re, im = spectrum[:count, cols], spectrum[count:, cols]
            even = jnp.where(is_left, re, pltpu.roll(im, width, 1))
            odd = jnp.where(is_left, pltpu.roll(re, width, 1), im)
            at = stream * rows + 2 * pair
            for (start, stop), out_ref in zip(splits, out_refs):
                out_ref[:, at, :] = even[start:stop]
                out_ref[:, at + 1, :] = odd[start:stop]


def transform(table, traces, sizes, after=()):
    src_local, rcv_local, samples = traces.shape
    streams, rows = STREAMS, STREAM_ROWS
    step = streams * rows
    splits, start = [], 0
    for size in sizes:
        splits.append((start, start + size))
        start += size
    return pl.pallas_call(
        functools.partial(transform_kernel, tuple(splits), streams),
        grid=(src_local // step,),
        in_specs=[pl.BlockSpec(table.shape, lambda i: (0, 0))]
        + [
            pl.BlockSpec((rows, rcv_local, samples), lambda i, k=k: (streams * i + k, 0, 0))
            for k in range(streams)
        ]
        + [pl.BlockSpec(memory_space=pl.ANY)] * len(after),
        out_specs=[pl.BlockSpec((size, step, LANES), lambda i: (0, i, 0)) for size in sizes],
        out_shape=[jax.ShapeDtypeStruct((size, src_local, LANES), F32) for size in sizes],
        compiler_params=params(),
        cost_estimate=cost(
            6 * 2 * start * src_local * rcv_local * samples,
            4 * traces.size + 4 * start * src_local * LANES,
        ),
        name="transform",
    )(table, *[traces] * streams, *after)


def split_table(freqs, samples):
    table = freq_table(freqs, samples)
    table = jnp.concatenate([table[:, 0], table[:, 1]], axis=0)
    high = lax.reduce_precision(table, 8, 7)
    return jnp.concatenate([high.astype(BF16), (table - high).astype(BF16)], axis=0)


def merge_kernel(core_ref, own_ref, other_ref, *refs):
    blocks = own_ref.shape[1]
    out_refs = refs[-1:] if len(refs[-1].shape) == 6 else refs[-blocks:]
    width = LANES // 2
    is_left = lax.broadcasted_iota(jnp.int32, (1, LANES), 1) < width
    is_first = core_ref[0] == 0
    for block in range(blocks):
        out_ref = out_refs[0].at[0, block] if len(out_refs) == 1 else out_refs[block].at[0]
        for item in range(own_ref.shape[2]):
            own, other = own_ref[0, block, item], other_ref[0, block, item]
            left = jnp.where(is_first, own, other)
            right = jnp.where(is_first, other, own)
            out_ref[item, 0] = jnp.where(is_left, left, pltpu.roll(right, width, 1))
            out_ref[item, 1] = jnp.where(is_left, pltpu.roll(left, width, 1), right)


def merge(core, own, other, start, count, by_src, after=()):
    n_src, n_z, _, rows, _ = own.shape
    spec = pl.BlockSpec((1, n_z, count, rows, LANES), lambda i, c: (i, 0, start // count, 0, 0))
    if by_src:
        out_specs = [pl.BlockSpec((1, n_z, count, 2, rows, LANES), lambda i, c: (i, 0, 0, 0, 0, 0))]
        out_shape = [jax.ShapeDtypeStruct((n_src, n_z, count, 2, rows, LANES), F32)]
    else:
        out_specs = [pl.BlockSpec((1, count, 2, rows, LANES), lambda i, c: (i, 0, 0, 0, 0))] * n_z
        out_shape = [jax.ShapeDtypeStruct((n_src, count, 2, rows, LANES), F32)] * n_z
    return pl.pallas_call(
        merge_kernel,
        grid_spec=pltpu.PrefetchScalarGridSpec(
            num_scalar_prefetch=1,
            grid=(n_src,),
            in_specs=[spec, spec] + [pl.BlockSpec(memory_space=pl.ANY)] * len(after),
            out_specs=out_specs,
        ),
        out_shape=out_shape,
        compiler_params=params(),
        cost_estimate=cost(0, 4 * 4 * n_src * n_z * count * rows * LANES),
        name="merge",
    )(core, own, other, *after)


def regroup_kernel(*refs):
    out_ref = refs[-1]
    blocks = out_ref.shape[1]
    for b in range(blocks):
        start = 0
        for ref in (refs[b], refs[blocks + b]):
            stop = start + ref.shape[1]
            out_ref[0, b, start:stop] = ref[0]
            start = stop


def regroup(part, other):
    n_src, _, *rest = part[0].shape
    count = part[0].shape[1] + other[0].shape[1]
    spec = lambda x: pl.BlockSpec((1,) + x.shape[1:], lambda i: (i, 0, 0, 0, 0))
    return pl.pallas_call(
        regroup_kernel,
        grid=(n_src,),
        in_specs=[spec(x) for x in (*part, *other)],
        out_specs=pl.BlockSpec((1, len(part), count, *rest), lambda i: (i, 0, 0, 0, 0, 0)),
        out_shape=jax.ShapeDtypeStruct((n_src, len(part), count, *rest), F32),
        compiler_params=params(),
        cost_estimate=cost(0, 8 * len(part) * (part[0].size + other[0].size)),
        name="regroup",
    )(*part, *other)


def pack_kernel(place_ref, block_ref, *out_refs):
    size = LANES
    z = place_ref[1]
    row = lax.broadcasted_iota(jnp.int32, (size, size), 0)
    col = lax.broadcasted_iota(jnp.int32, (size, size), 1)
    blocks = block_ref.shape[0]
    for offset, out_ref in enumerate(out_refs, 1):
        for k in range(1, blocks):
            for part in range(2):
                start = (2 * (k - 1) + part) * size
                out_ref[0, start : start + size, :] = block_ref[jnp.bitwise_xor(z, k), offset, 0, part]
        re, im = block_ref[z, offset, 0, 0], block_ref[z, offset, 0, 1]
        lower, upper = re + re.T, im + im.T
        start = 2 * (blocks - 1) * size
        both = jnp.where(row > col, lower, jnp.where(row < col, upper, re))
        out_ref[0, start : start + size, :] = both
        diagonal = jnp.sum(jnp.where(row == col, im, 0.0), axis=0, keepdims=True)
        out_ref[0, start + size :, :] = jnp.broadcast_to(diagonal, (8, size))


def pack(place, blocks):
    n_src, n_z, count, _, size, _ = blocks.shape
    rows = (2 * (n_src - 1) + 1) * size + 8
    return pl.pallas_call(
        pack_kernel,
        grid_spec=pltpu.PrefetchScalarGridSpec(
            num_scalar_prefetch=1,
            grid=(count,),
            in_specs=[pl.BlockSpec((n_src, n_z, 1, 2, size, size), lambda j, s: (0, 0, j, 0, 0, 0))],
            out_specs=[pl.BlockSpec((1, rows, size), lambda j, s: (j, 0, 0))] * (n_z - 1),
        ),
        out_shape=[jax.ShapeDtypeStruct((count, rows, size), F32)] * (n_z - 1),
        compiler_params=params(),
        cost_estimate=cost(0, 4 * 2 * blocks.size),
        name="pack",
    )(place, blocks)


def place_packed(u_ref, place_ref, own_ref, *far_refs):
    size = LANES
    z = place_ref[1]
    row = lax.broadcasted_iota(jnp.int32, (size, size), 0)
    col = lax.broadcasted_iota(jnp.int32, (size, size), 1)
    blocks = own_ref.shape[0]
    for part in range(2):
        for source in range(blocks):
            u_ref[part, z, source * size : (source + 1) * size, :] = own_ref[source, 0, 0, part]
    for offset, far_ref in enumerate(far_refs, 1):
        there = jnp.bitwise_xor(z, offset)
        for k in range(1, blocks):
            at = pl.ds(pl.multiple_of(jnp.bitwise_xor(there, k) * size, size), size)
            for part in range(2):
                start = (2 * (k - 1) + part) * size
                u_ref[part, there, at, :] = far_ref[0, start : start + size, :]
        at = pl.ds(pl.multiple_of(there * size, size), size)
        start = 2 * (blocks - 1) * size
        both = far_ref[0, start : start + size, :]
        diagonal = far_ref[0, start + size : start + size + 1, :]
        u_ref[0, there, at, :] = jnp.where(row >= col, both, 0.0)
        u_ref[1, there, at, :] = jnp.where(row < col, both, jnp.where(row == col, diagonal, 0.0))


def solve_one(u_ref, data_ref, weight, primaries_ref, resid_ref, pred_ref, sums_ref, is_first, before_ref):
    size = LANES
    blocks = u_ref.shape[1]
    for part in range(2):
        for i in range(blocks):
            for k in range(i, blocks):
                here = slice(i * size, (i + 1) * size)
                there = slice(k * size, (k + 1) * size)
                block = 0.5 * (u_ref[part, k, here, :] + u_ref[part, i, there, :].T)
                data_ref[part, here, there] = block
                if k > i:
                    data_ref[part, there, here] = block.T
    data_re, data_im = data_ref[0], data_ref[1]
    re, im, both = halves(data_re), halves(data_im), halves(data_re + data_im)
    prim_re, prim_im = primaries_ref[0, 0], primaries_ref[0, 1]
    first = product(halves(prim_re), re)
    second = product(halves(prim_im), im)
    third = product(halves(prim_re + prim_im), both)
    resid_re = data_re - (first - second)
    resid_im = data_im - (third - first - second)
    resid_ref[0, 0] = resid_re
    resid_ref[0, 1] = resid_im
    cross = product(re, im)
    gram_re = product(re, re) + product(im, im)
    gram_im = cross - cross.T
    first = product(halves(resid_re), halves(gram_re))
    second = product(halves(resid_im), halves(gram_im))
    third = product(halves(resid_re + resid_im), halves(gram_re + gram_im))
    pred_re = first - second
    pred_im = third - first - second
    pred_ref[0, 0] = pred_re
    pred_ref[0, 1] = pred_im

    def fold(x):
        x = x.reshape(x.shape[0] // 8, 8, x.shape[1]).sum(0)
        return sum(x[:, k * LANES : (k + 1) * LANES] for k in range(x.shape[1] // LANES))

    numer = weight * fold(resid_re * pred_re + resid_im * pred_im)
    denom = weight * fold(pred_re * pred_re + pred_im * pred_im)

    @pl.when(is_first)
    def _():
        sums_ref[...] = jnp.zeros_like(sums_ref) if before_ref is None else before_ref[...]

    sums_ref[0] += numer
    sums_ref[1] += denom


def place_raw(u_ref, place_ref, block_ref):
    size = LANES
    z = place_ref[1]
    for source in range(block_ref.shape[0]):
        for b in range(block_ref.shape[1]):
            for part in range(2):
                rows = slice(source * size, (source + 1) * size)
                u_ref[part, jnp.bitwise_xor(z, b), rows, :] = block_ref[source, b, 0, part]


def solve_kernel(offset, n_arrived, n_before, place_ref, weight_ref, primaries_ref, *refs):
    before_ref = refs[n_arrived + 2] if n_before else None
    resid_ref, pred_ref, sums_ref, u_ref, data_ref = refs[-5:]
    j = pl.program_id(0)
    if n_arrived == 1:
        place_raw(u_ref, place_ref, refs[0])
    else:
        place_packed(u_ref, place_ref, *refs[:n_arrived])
    solve_one(u_ref, data_ref, weight_ref[offset + j], primaries_ref, resid_ref, pred_ref, sums_ref, j == 0, before_ref)


def solve(place, weights, primaries, arrived, offset, before, after=()):
    size = LANES
    _, _, n, m = primaries.shape
    n_src, n_z, count = arrived[0].shape[:3]
    freq = pl.BlockSpec((1, 2, n, m), lambda j, s: (offset + j, 0, 0, 0))
    if len(arrived) == 1:
        specs = [pl.BlockSpec((n_src, n_z, 1, 2, size, size), lambda j, s: (0, 0, j, 0, 0, 0))]
    else:
        specs = [pl.BlockSpec((n_src, 1, 1, 2, size, size), lambda j, s: (0, 0, j, 0, 0, 0))]
        specs += [pl.BlockSpec((1,) + x.shape[1:], lambda j, s: (j, 0, 0)) for x in arrived[1:]]
    sums = pl.BlockSpec((2, 8, LANES), lambda j, s: (0, 0, 0))
    n_before = len(before)
    anywhere = pl.BlockSpec(memory_space=pl.ANY)
    at = 3 + len(specs)
    return pl.pallas_call(
        functools.partial(solve_kernel, offset, len(specs), n_before),
        grid_spec=pltpu.PrefetchScalarGridSpec(
            num_scalar_prefetch=1,
            grid=(count,),
            in_specs=[pl.BlockSpec(memory_space=pltpu.SMEM), freq]
            + specs
            + ([anywhere, anywhere, sums] if n_before else [])
            + [anywhere] * len(after),
            out_specs=[freq, freq, sums],
            scratch_shapes=[
                pltpu.VMEM((2, n // size, n, size), F32),
                pltpu.VMEM((2, n, m), F32),
            ],
        ),
        out_shape=[
            jax.ShapeDtypeStruct(primaries.shape, F32),
            jax.ShapeDtypeStruct(primaries.shape, F32),
            jax.ShapeDtypeStruct((2, 8, LANES), F32),
        ],
        input_output_aliases={at: 0, at + 1: 1} if n_before else {},
        compiler_params=params(),
        cost_estimate=cost(count * 27 * 2 * n * n * m, count * 4 * 2 * n * m * 4),
        name="solve",
    )(place, weights, primaries, *arrived, *before, *after)


def update_kernel(sums_ref, resid_ref, pred_ref, out_ref):
    total = jnp.sum(sums_ref[...], axis=0)
    step = jnp.sum(total[0], keepdims=True) / jnp.sum(total[1], keepdims=True)
    out_ref[...] = resid_ref[...] - step[None, None] * pred_ref[...]


def update(sums, resid, pred):
    count, _, n, m = resid.shape
    rows = pl.BlockSpec((1, 2, n, m), lambda i: (i, 0, 0, 0))
    return pl.pallas_call(
        update_kernel,
        grid=(count,),
        in_specs=[pl.BlockSpec(sums.shape, lambda i: (0, 0, 0, 0)), rows, rows],
        out_specs=rows,
        out_shape=jax.ShapeDtypeStruct(resid.shape, F32),
        compiler_params=pltpu.CompilerParams(vmem_limit_bytes=UPDATE_VMEM_BYTES),
        cost_estimate=cost(2 * resid.size, 12 * resid.size),
        name="update",
    )(sums, resid, pred)


def by_offset(values, n_src, n_rcv):
    bits = n_rcv.bit_length() - 1
    rcv = lax.axis_index("rcv")
    values = values.reshape((n_src,) + (2,) * bits + (-1,))
    for axis in range(bits):
        bit = (rcv >> (bits - 1 - axis)) & 1
        values = jnp.where(bit == 1, jnp.flip(values, axis + 1), values)
    return values.reshape(n_src, n_rcv // 2, 2, -1)


def fence(*arrays):
    return lax.optimization_barrier(arrays)


def chunks_of(freq_local):
    edges = [k * freq_local // 4 for k in range(5)]
    return list(zip(edges[:-1], edges[1:]))


def paired_step(traces, freq_index, primaries):
    src_local, rcv_local, samples = traces.shape
    n_src, n_rcv = lax.axis_size("src"), lax.axis_size("rcv")
    n_z = n_rcv // 2
    freq_local = primaries.shape[0]
    src, rcv = lax.axis_index("src"), lax.axis_index("rcv")
    z, core = rcv // 2, rcv % 2
    place = jnp.stack([src, z]).astype(jnp.int32)
    core_id = core.reshape(1).astype(jnp.int32)

    def along(x, offset):
        return lax.ppermute(x, "rcv", [(i, i ^ offset) for i in range(n_rcv)])

    def along_src(x):
        return lax.all_to_all(x, "src", split_axis=0, concat_axis=0, tiled=True)

    def along_z(blocks):
        return [blocks[0]] + [along(blocks[b], 2 * b) for b in range(1, n_z)]

    chunks = chunks_of(freq_local)
    freqs = by_offset(freq_index, n_src, n_rcv)
    freqs = jnp.transpose(freqs, (2, 0, 1, 3))

    def transformed(groups, after=(), swap=True):
        rows = jnp.concatenate([freqs[..., a:b].reshape(-1) for a, b in groups])
        sizes = [n_src * n_z * (b - a) for a, b in groups for _ in range(2)]
        outs = transform(split_table(rows, samples), traces, sizes, after)
        outs = [x.reshape(n_src, n_z, -1, src_local, LANES) for x in outs]
        pairs = [(outs[2 * i], outs[2 * i + 1]) for i in range(len(groups))]
        return [(own, along(away, 1) if swap else away) for own, away in pairs]

    weights = freq_index.astype(jnp.float32) / (samples // 2)
    weights = lax.dynamic_slice_in_dim(weights, (src * n_rcv + rcv) * freq_local, freq_local)

    a, b, c, d = chunks
    size = [stop - start for start, stop in chunks]
    middle = (a[0] + a[1]) // 2
    a1, a2 = (a[0], middle), (middle, a[1])
    spec_a1, spec_b, spec_a2, spec_c = transformed([a1, b, a2, c])
    first_a1 = merge(core_id, *spec_a1, 0, a1[1] - a1[0], False)
    sent_b = merge(core_id, *spec_b, 0, size[1], True, (first_a1[0],))[0]
    *first_a1, sent_b = fence(*first_a1, sent_b)

    raw_a1 = along_z(first_a1)
    arrived_b = along_src(sent_b)
    first_a2 = merge(core_id, *spec_a2, 0, a2[1] - a2[0], False, (sent_b,))
    sent_c = merge(core_id, *spec_c, 0, size[2], True, (sent_b,))[0]
    (spec_d,) = transformed([d], (sent_b,), False)
    *raw_a1, arrived_b, sent_c, own_d, away_d = fence(*raw_a1, arrived_b, sent_c, *spec_d)

    *first_a2, _ = fence(*first_a2, sent_c)
    raw_a2 = along_z(first_a2)
    arrived_c = along_src(sent_c)
    packed_b = pack(place, arrived_b)
    sent_d = merge(core_id, own_d, along(away_d, 1), 0, size[3], True)[0]
    *all_a, arrived_b, arrived_c, sent_d, x, y, w = fence(*raw_a1, *raw_a2, arrived_b, arrived_c, sent_d, *packed_b)

    here_b = along_z([arrived_b, x, y, w])
    arrived_d = along_src(sent_d)
    packed_c = pack(place, arrived_c)
    whole_a = regroup(all_a[:n_z], all_a[n_z:])
    *here_b, arrived_c, arrived_d, whole_a, x, y, w = fence(*here_b, arrived_c, arrived_d, whole_a, *packed_c)

    here_c = along_z([arrived_c, x, y, w])
    whole_a = along_src(whole_a)
    packed_d = pack(place, arrived_d)
    before = solve(place, weights, primaries, here_b, b[0], ())
    *here_c, arrived_d, whole_a, x, y, w, r, p, q = fence(*here_c, arrived_d, whole_a, *packed_d, *before)

    here_d = along_z([arrived_d, x, y, w])
    before = solve(place, weights, primaries, [whole_a], a[0], (r, p, q))
    before = solve(place, weights, primaries, here_c, c[0], before)
    *here_d, r, p, q = fence(*here_d, *before)
    before = solve(place, weights, primaries, here_d, d[0], (r, p, q))

    resid, pred, sums = before
    n_all = n_src * n_rcv
    sums = jnp.broadcast_to(sums[None], (n_all,) + sums.shape)
    sums = lax.all_to_all(sums, AXES, split_axis=0, concat_axis=0, tiled=True)
    return (resid, update(sums, resid, pred))


def solution(mesh):
    in_specs = (P("src", "rcv", None), P(), P(("src", "rcv"), None, None, None))
    out_specs = (P(("src", "rcv"), None, None, None), P(("src", "rcv"), None, None, None))
    n_src, n_rcv = mesh.shape["src"], mesh.shape["rcv"]

    def step(traces, freq_index, primaries):
        src_local, rcv_local, _ = traces.shape
        square = src_local == LANES and 2 * rcv_local == LANES
        if square and n_src == 4 and n_rcv == 2 * n_src and primaries.shape[0] >= 8:
            return paired_step(traces, freq_index, primaries)
        return plain_step(traces, freq_index, primaries)

    return jax.shard_map(step, mesh=mesh, in_specs=in_specs, out_specs=out_specs, check_vma=False)
```

```python
import functools
import math

import jax
import jax.numpy as jnp
from jax import lax
from jax.experimental import pallas as pl
from jax.experimental.pallas import tpu as pltpu
from jax.sharding import PartitionSpec as P

AXES = ("src", "rcv")
LANES = 128
COST_SCALE = 100
VMEM_BYTES = 56 * 1024 * 1024
SMALL_VMEM_BYTES = 14 * 1024 * 1024
F32 = jnp.float32
BF16 = jnp.bfloat16


def freq_table(freq_index, samples):
    times = jnp.arange(samples, dtype=jnp.int32)
    phase = freq_index[:, None] * times[None, :] % samples
    angle = phase.astype(jnp.float32) * (2.0 * math.pi / samples)
    return jnp.stack([jnp.cos(angle), -jnp.sin(angle)], axis=1) / math.sqrt(samples)


def matrix_product(left, right):
    return jnp.einsum("fij,fjk->fik", left, right, precision=lax.Precision.HIGHEST)


def complex_product(left_re, left_im, right_re, right_im, adjoint):
    if adjoint:
        right_re = jnp.swapaxes(right_re, 1, 2)
        right_im = -jnp.swapaxes(right_im, 1, 2)
    real_part = matrix_product(left_re, right_re) - matrix_product(left_im, right_im)
    imag_part = matrix_product(left_re, right_im) + matrix_product(left_im, right_re)
    return (real_part, imag_part)


def plain_step(traces, freq_index, primaries):
    src_local, rcv_local, samples = traces.shape
    n_src = lax.axis_size("src")
    n_rcv = lax.axis_size("rcv")
    table = freq_table(freq_index, samples)
    flat = traces.reshape(src_local * rcv_local, samples)
    spectrum = lax.dot_general(
        table,
        flat,
        (((2,), (1,)), ((), ())),
        precision=lax.Precision.HIGHEST,
        preferred_element_type=jnp.float32,
    )
    spectrum = spectrum[None]
    freq_local = primaries.shape[0]
    arrived = lax.all_to_all(spectrum, AXES, split_axis=1, concat_axis=0, tiled=True)
    arrived = arrived.reshape(n_src, n_rcv, freq_local, 2, src_local, rcv_local)
    arrived = jnp.transpose(arrived, (2, 3, 0, 4, 1, 5))
    whole = arrived.reshape(freq_local, 2, n_src * src_local, n_rcv * rcv_local)
    data_re = 0.5 * (whole[:, 0] + jnp.swapaxes(whole[:, 0], 1, 2))
    data_im = 0.5 * (whole[:, 1] + jnp.swapaxes(whole[:, 1], 1, 2))
    model_re, model_im = complex_product(primaries[:, 0], primaries[:, 1], data_re, data_im, False)
    resid_re = data_re - model_re
    resid_im = data_im - model_im
    grad_re, grad_im = complex_product(resid_re, resid_im, data_re, data_im, True)
    pred_re, pred_im = complex_product(grad_re, grad_im, data_re, data_im, False)
    offset = (lax.axis_index("src") * n_rcv + lax.axis_index("rcv")) * freq_local
    weights = freq_index.astype(jnp.float32) / (samples // 2)
    weights = lax.dynamic_slice_in_dim(weights, offset, freq_local)
    scaled = weights[:, None, None]
    numer = jnp.sum(scaled * (resid_re * pred_re + resid_im * pred_im))
    denom = jnp.sum(scaled * (pred_re * pred_re + pred_im * pred_im))
    numer, denom = lax.psum((numer, denom), AXES)
    step_size = numer / denom
    resid = jnp.stack([resid_re, resid_im], 1)
    pred = jnp.stack([pred_re, pred_im], 1)
    return (resid, resid - step_size * pred)


def params(vmem_bytes=VMEM_BYTES):
    return pltpu.CompilerParams(vmem_limit_bytes=vmem_bytes)


def cost(flops, moved):
    return pl.CostEstimate(flops=int(flops) // COST_SCALE, bytes_accessed=int(moved) // COST_SCALE, transcendentals=0)


def halves(x):
    high = x.astype(BF16)
    return high, (x - high.astype(F32)).astype(BF16)


def product(left, right):
    dot = functools.partial(jnp.dot, preferred_element_type=F32)
    return dot(left[0], right[0]) + (dot(left[0], right[1]) + dot(left[1], right[0]))


def fill_table(table_ref, freq_ref, samples):
    count = freq_ref.shape[0]
    freq = freq_ref[...]
    lane = lax.broadcasted_iota(jnp.int32, (count, LANES), 1)

    def turn(phase):
        angle = (phase & (samples - 1)).astype(F32) * (2.0 * math.pi / samples)
        return jnp.cos(angle), jnp.sin(angle)

    fine_cos, fine_sin = turn(freq * lane)
    coarse_cos, coarse_sin = turn(freq * (lane * LANES))
    scale = 1.0 / math.sqrt(samples)
    for a in range(samples // LANES):
        cos_a, sin_a = coarse_cos[:, a : a + 1] * scale, coarse_sin[:, a : a + 1] * scale
        cols = slice(a * LANES, (a + 1) * LANES)
        re = halves(cos_a * fine_cos - sin_a * fine_sin)
        im = halves(-(sin_a * fine_cos + cos_a * fine_sin))
        for half in range(2):
            table_ref[2 * half * count : (2 * half + 1) * count, cols] = re[half]
            table_ref[(2 * half + 1) * count : (2 * half + 2) * count, cols] = im[half]


def transform_kernel(splits, freq_ref, traces_ref, *refs):
    out_refs, table_ref = refs[-len(splits) - 1 : -1], refs[-1]
    rows, width, samples = traces_ref.shape
    count = freq_ref.shape[0]

    @pl.when(pl.program_id(0) == 0)
    def _():
        fill_table(table_ref, freq_ref, samples)

    is_left = lax.broadcasted_iota(jnp.int32, (1, LANES), 1) < width
    contract = (((1,), (1,)), ((), ()))
    x = traces_ref[...].reshape(rows * width, samples)
    high, low = halves(x)
    first = lax.dot_general(table_ref[...], high, contract, preferred_element_type=F32)
    second = lax.dot_general(table_ref[: 2 * count], low, contract, preferred_element_type=F32)
    spectrum = first[: 2 * count] + first[2 * count :] + second
    for group in range(rows // 8):
        slabs = []
        for pair in range(4 * group, 4 * group + 4):
            cols = slice(pair * LANES, (pair + 1) * LANES)
            re, im = spectrum[:count, cols], spectrum[count:, cols]
            slabs.append(jnp.where(is_left, re, pltpu.roll(im, width, 1)))
            slabs.append(jnp.where(is_left, pltpu.roll(re, width, 1), im))
        turned = jnp.swapaxes(jnp.stack(slabs, 0), 0, 1)
        for (start, stop), out_ref in zip(splits, out_refs):
            out_ref[:, 8 * group : 8 * group + 8, :] = turned[start:stop]


def transform(freqs, traces, sizes, after=()):
    src_local, rcv_local, samples = traces.shape
    step = min(src_local, 16)
    splits, start = [], 0
    for size in sizes:
        splits.append((start, start + size))
        start += size
    return pl.pallas_call(
        functools.partial(transform_kernel, tuple(splits)),
        grid=(src_local // step,),
        in_specs=[
            pl.BlockSpec((start, 1), lambda i: (0, 0)),
            pl.BlockSpec((step, rcv_local, samples), lambda i: (i, 0, 0)),
        ]
        + [pl.BlockSpec(memory_space=pl.ANY)] * len(after),
        out_specs=[pl.BlockSpec((size, step, LANES), lambda i: (0, i, 0)) for size in sizes],
        out_shape=[jax.ShapeDtypeStruct((size, src_local, LANES), F32) for size in sizes],
        scratch_shapes=[pltpu.VMEM((4 * start, samples), BF16)],
        compiler_params=params(),
        cost_estimate=cost(
            6 * 2 * start * src_local * rcv_local * samples,
            4 * traces.size + 4 * start * src_local * LANES,
        ),
        name="transform",
    )(freqs.reshape(-1, 1), traces, *after)


def merge_kernel(core_ref, own_ref, other_ref, *refs):
    blocks = own_ref.shape[1]
    out_refs = refs[-1:] if len(refs[-1].shape) == 6 else refs[-blocks:]
    width = LANES // 2
    is_left = lax.broadcasted_iota(jnp.int32, (1, LANES), 1) < width
    is_first = core_ref[0] == 0
    for block in range(blocks):
        out_ref = out_refs[0].at[0, block] if len(out_refs) == 1 else out_refs[block].at[0]
        for item in range(own_ref.shape[2]):
            own, other = own_ref[0, block, item], other_ref[0, block, item]
            left = jnp.where(is_first, own, other)
            right = jnp.where(is_first, other, own)
            out_ref[item, 0] = jnp.where(is_left, left, pltpu.roll(right, width, 1))
            out_ref[item, 1] = jnp.where(is_left, pltpu.roll(left, width, 1), right)


def merge(core, own, other, start, count, by_src, after=()):
    n_src, n_z, _, rows, _ = own.shape
    spec = pl.BlockSpec((1, n_z, count, rows, LANES), lambda i, c: (i, 0, start // count, 0, 0))
    if by_src:
        out_specs = [pl.BlockSpec((1, n_z, count, 2, rows, LANES), lambda i, c: (i, 0, 0, 0, 0, 0))]
        out_shape = [jax.ShapeDtypeStruct((n_src, n_z, count, 2, rows, LANES), F32)]
    else:
        out_specs = [pl.BlockSpec((1, count, 2, rows, LANES), lambda i, c: (i, 0, 0, 0, 0))] * n_z
        out_shape = [jax.ShapeDtypeStruct((n_src, count, 2, rows, LANES), F32)] * n_z
    return pl.pallas_call(
        merge_kernel,
        grid_spec=pltpu.PrefetchScalarGridSpec(
            num_scalar_prefetch=1,
            grid=(n_src,),
            in_specs=[spec, spec] + [pl.BlockSpec(memory_space=pl.ANY)] * len(after),
            out_specs=out_specs,
        ),
        out_shape=out_shape,
        compiler_params=params(SMALL_VMEM_BYTES),
        cost_estimate=cost(0, 4 * 4 * n_src * n_z * count * rows * LANES),
        name="merge",
    )(core, own, other, *after)


def regroup_kernel(*refs):
    out_ref = refs[-1]
    blocks = out_ref.shape[1]
    for b in range(blocks):
        start = 0
        for ref in (refs[b], refs[blocks + b]):
            stop = start + ref.shape[1]
            out_ref[0, b, start:stop] = ref[0]
            start = stop


def regroup(part, other):
    n_src, _, *rest = part[0].shape
    count = part[0].shape[1] + other[0].shape[1]
    spec = lambda x: pl.BlockSpec((1,) + x.shape[1:], lambda i: (i, 0, 0, 0, 0))
    return pl.pallas_call(
        regroup_kernel,
        grid=(n_src,),
        in_specs=[spec(x) for x in (*part, *other)],
        out_specs=pl.BlockSpec((1, len(part), count, *rest), lambda i: (i, 0, 0, 0, 0, 0)),
        out_shape=jax.ShapeDtypeStruct((n_src, len(part), count, *rest), F32),
        compiler_params=params(SMALL_VMEM_BYTES),
        cost_estimate=cost(0, 8 * len(part) * (part[0].size + other[0].size)),
        name="regroup",
    )(*part, *other)


def beside_kernel(place_ref, block_ref, out_ref):
    out_ref[...] = block_ref[0, :, :, 0]


def beside(place, blocks):
    _, n_z, count, _, size, _ = blocks.shape
    return pl.pallas_call(
        beside_kernel,
        grid_spec=pltpu.PrefetchScalarGridSpec(
            num_scalar_prefetch=1,
            grid=(1,),
            in_specs=[
                pl.BlockSpec(
                    (1, n_z // 2, count, 1, size, size),
                    lambda i, s: (jnp.bitwise_xor(s[1], 1), 1, 0, 1 - s[1] % 2, 0, 0),
                )
            ],
            out_specs=pl.BlockSpec((n_z // 2, count, size, size), lambda i, s: (0, 0, 0, 0)),
        ),
        out_shape=jax.ShapeDtypeStruct((n_z // 2, count, size, size), F32),
        compiler_params=params(SMALL_VMEM_BYTES),
        cost_estimate=cost(0, 4 * n_z * count * size * size),
        name="beside",
    )(place, blocks)


def put_diagonal(out_ref, start, re, im):
    size = re.shape[0]
    row = lax.broadcasted_iota(jnp.int32, (size, size), 0)
    col = lax.broadcasted_iota(jnp.int32, (size, size), 1)
    lower, upper = re + re.T, im + im.T
    both = jnp.where(row > col, lower, jnp.where(row < col, upper, re))
    out_ref[0, start : start + size, :] = both
    diagonal = jnp.sum(jnp.where(row == col, im, 0.0), axis=0, keepdims=True)
    out_ref[0, start + size :, :] = jnp.broadcast_to(diagonal, (8, size))


def pack_kernel(place_ref, block_ref, near_ref, *far_refs):
    size = LANES
    z = place_ref[1]
    for k in range(1, 4):
        for part in range(2):
            start = (2 * (k - 1) + part) * size
            near_ref[0, start : start + size, :] = block_ref[jnp.bitwise_xor(z, k), 1, 0, part]
    put_diagonal(near_ref, 6 * size, block_ref[z, 1, 0, 0], block_ref[z, 1, 0, 1])
    other_half = 2 * (1 - z // 2)
    for far, far_ref in enumerate(far_refs):
        for part in range(2):
            for k in range(2):
                start = (2 * part + k) * size
                far_ref[0, start : start + size, :] = block_ref[other_half + k, 2 + far, 0, part]
        put_diagonal(far_ref, 5 * size, block_ref[z, 2 + far, 0, 0], block_ref[z, 2 + far, 0, 1])


def pack(place, blocks, start, count):
    n_src, n_z, _, _, size, _ = blocks.shape
    near, far = 7 * size + 8, 6 * size + 8
    return pl.pallas_call(
        pack_kernel,
        grid_spec=pltpu.PrefetchScalarGridSpec(
            num_scalar_prefetch=1,
            grid=(count,),
            in_specs=[pl.BlockSpec((n_src, n_z, 1, 2, size, size), lambda j, s: (0, 0, start + j, 0, 0, 0))],
            out_specs=[pl.BlockSpec((1, rows, size), lambda j, s: (j, 0, 0)) for rows in (near, far, far)],
        ),
        out_shape=[jax.ShapeDtypeStruct((count, rows, size), F32) for rows in (near, far, far)],
        compiler_params=params(SMALL_VMEM_BYTES),
        cost_estimate=cost(0, 4 * 2 * blocks.size),
        name="pack",
    )(place, blocks)


def add_beside_kernel(place_ref, block_ref, swapped_ref, *refs):
    for far, far_ref in enumerate(refs[-2:]):
        for j in range(far_ref.shape[0]):
            far_ref[j] = block_ref[0, far, j, 0] + swapped_ref[1 - far, j].T


def add_beside(place, blocks, swapped, packed, start):
    size = LANES
    near, *fars = packed
    count = near.shape[0]
    spec = pl.BlockSpec((count, size, size), lambda i, s: (0, 4, 0))
    anywhere = pl.BlockSpec(memory_space=pl.ANY)
    fars = pl.pallas_call(
        add_beside_kernel,
        grid_spec=pltpu.PrefetchScalarGridSpec(
            num_scalar_prefetch=1,
            grid=(1,),
            in_specs=[
                pl.BlockSpec(
                    (1, 2, count, 1, size, size),
                    lambda i, s: (jnp.bitwise_xor(s[1], 1), 1, start // count, s[1] % 2, 0, 0),
                ),
                pl.BlockSpec((2, count, size, size), lambda i, s: (0, start // count, 0, 0)),
                anywhere,
                anywhere,
            ],
            out_specs=[spec, spec],
        ),
        out_shape=[jax.ShapeDtypeStruct(x.shape, F32) for x in fars],
        input_output_aliases={3: 0, 4: 1},
        compiler_params=params(SMALL_VMEM_BYTES),
        cost_estimate=cost(0, 4 * 6 * count * size * size),
        name="add_beside",
    )(place, blocks, swapped, *fars)
    return [near, *fars]


def take_diagonal(u_ref, there, packed_ref, start):
    size = LANES
    row = lax.broadcasted_iota(jnp.int32, (size, size), 0)
    col = lax.broadcasted_iota(jnp.int32, (size, size), 1)
    at = pl.ds(pl.multiple_of(there * size, size), size)
    both = packed_ref[0, start : start + size, :]
    diagonal = packed_ref[0, start + size : start + size + 1, :]
    u_ref[0, there, at, :] = jnp.where(row >= col, both, 0.0)
    u_ref[1, there, at, :] = jnp.where(row < col, both, jnp.where(row == col, diagonal, 0.0))


def place_packed(u_ref, place_ref, own_ref, near_ref, *far_refs):
    size = LANES
    z = place_ref[1]
    for part in range(2):
        for source in range(4):
            u_ref[part, z, source * size : (source + 1) * size, :] = own_ref[source, 0, 0, part]
    there = jnp.bitwise_xor(z, 1)
    for k in range(1, 4):
        at = pl.ds(pl.multiple_of(jnp.bitwise_xor(there, k) * size, size), size)
        for part in range(2):
            start = (2 * (k - 1) + part) * size
            u_ref[part, there, at, :] = near_ref[0, start : start + size, :]
    take_diagonal(u_ref, there, near_ref, 6 * size)
    half = pl.ds(pl.multiple_of((z // 2) * 2 * size, size), 2 * size)
    for far, far_ref in enumerate(far_refs):
        there = jnp.bitwise_xor(z, 2 + far)
        for part in range(2):
            u_ref[part, there, half, :] = far_ref[0, 2 * part * size : 2 * (part + 1) * size, :]
        at = pl.ds(pl.multiple_of(jnp.bitwise_xor(there, 1) * size, size), size)
        summed = far_ref[0, 4 * size : 5 * size, :]
        is_re = there % 2 == 0
        u_ref[0, there, at, :] = jnp.where(is_re, summed, 0.0)
        u_ref[1, there, at, :] = jnp.where(is_re, 0.0, summed)
        take_diagonal(u_ref, there, far_ref, 5 * size)


def solve_one(u_ref, data_ref, weight, primaries_ref, resid_ref, pred_ref, sums_ref, is_first, before_ref):
    size = LANES
    blocks = u_ref.shape[1]
    for part in range(2):
        for i in range(blocks):
            for k in range(i, blocks):
                here = slice(i * size, (i + 1) * size)
                there = slice(k * size, (k + 1) * size)
                block = 0.5 * (u_ref[part, k, here, :] + u_ref[part, i, there, :].T)
                data_ref[part, here, there] = block
                if k > i:
                    data_ref[part, there, here] = block.T
    data_re, data_im = data_ref[0], data_ref[1]
    re, im, both = halves(data_re), halves(data_im), halves(data_re + data_im)
    prim_re, prim_im = primaries_ref[0, 0], primaries_ref[0, 1]
    first = product(halves(prim_re), re)
    second = product(halves(prim_im), im)
    third = product(halves(prim_re + prim_im), both)
    resid_re = data_re - (first - second)
    resid_im = data_im - (third - first - second)
    resid_ref[0, 0] = resid_re
    resid_ref[0, 1] = resid_im
    cross = product(re, im)
    gram_re = product(re, re) + product(im, im)
    gram_im = cross - cross.T
    first = product(halves(resid_re), halves(gram_re))
    second = product(halves(resid_im), halves(gram_im))
    third = product(halves(resid_re + resid_im), halves(gram_re + gram_im))
    pred_re = first - second
    pred_im = third - first - second
    pred_ref[0, 0] = pred_re
    pred_ref[0, 1] = pred_im

    def fold(x):
        x = x.reshape(x.shape[0] // 8, 8, x.shape[1]).sum(0)
        return sum(x[:, k * LANES : (k + 1) * LANES] for k in range(x.shape[1] // LANES))

    numer = weight * fold(resid_re * pred_re + resid_im * pred_im)
    denom = weight * fold(pred_re * pred_re + pred_im * pred_im)

    @pl.when(is_first)
    def _():
        sums_ref[...] = jnp.zeros_like(sums_ref) if before_ref is None else before_ref[...]

    sums_ref[0] += numer
    sums_ref[1] += denom


def place_raw(u_ref, place_ref, block_ref):
    size = LANES
    z = place_ref[1]
    for source in range(block_ref.shape[0]):
        for b in range(block_ref.shape[1]):
            for part in range(2):
                rows = slice(source * size, (source + 1) * size)
                u_ref[part, jnp.bitwise_xor(z, b), rows, :] = block_ref[source, b, 0, part]


def solve_kernel(offset, n_arrived, n_before, place_ref, weight_ref, primaries_ref, *refs):
    before_ref = refs[n_arrived + 2] if n_before else None
    resid_ref, pred_ref, sums_ref, u_ref, data_ref = refs[-5:]
    j = pl.program_id(0)
    if n_arrived == 1:
        place_raw(u_ref, place_ref, refs[0])
    else:
        place_packed(u_ref, place_ref, *refs[:n_arrived])
    solve_one(u_ref, data_ref, weight_ref[offset + j], primaries_ref, resid_ref, pred_ref, sums_ref, j == 0, before_ref)


def solve(place, weights, primaries, arrived, offset, before, start=0):
    size = LANES
    _, _, n, m = primaries.shape
    n_src, n_z = arrived[0].shape[:2]
    count = arrived[-1].shape[2 if len(arrived) == 1 else 0]
    freq = pl.BlockSpec((1, 2, n, m), lambda j, s: (offset + j, 0, 0, 0))
    if len(arrived) == 1:
        specs = [pl.BlockSpec((n_src, n_z, 1, 2, size, size), lambda j, s: (0, 0, j, 0, 0, 0))]
    else:
        specs = [pl.BlockSpec((n_src, 1, 1, 2, size, size), lambda j, s: (0, 0, start + j, 0, 0, 0))]
        specs += [pl.BlockSpec((1,) + x.shape[1:], lambda j, s: (j, 0, 0)) for x in arrived[1:]]
    sums = pl.BlockSpec((2, 8, LANES), lambda j, s: (0, 0, 0))
    n_before = len(before)
    anywhere = pl.BlockSpec(memory_space=pl.ANY)
    at = 3 + len(specs)
    return pl.pallas_call(
        functools.partial(solve_kernel, offset, len(specs), n_before),
        grid_spec=pltpu.PrefetchScalarGridSpec(
            num_scalar_prefetch=1,
            grid=(count,),
            in_specs=[pl.BlockSpec(memory_space=pltpu.SMEM), freq]
            + specs
            + ([anywhere, anywhere, sums] if n_before else []),
            out_specs=[freq, freq, sums],
            scratch_shapes=[
                pltpu.VMEM((2, n // size, n, size), F32),
                pltpu.VMEM((2, n, m), F32),
            ],
        ),
        out_shape=[
            jax.ShapeDtypeStruct(primaries.shape, F32),
            jax.ShapeDtypeStruct(primaries.shape, F32),
            jax.ShapeDtypeStruct((2, 8, LANES), F32),
        ],
        input_output_aliases={at: 0, at + 1: 1} if n_before else {},
        compiler_params=params(),
        cost_estimate=cost(count * 27 * 2 * n * n * m, count * 4 * 2 * n * m * 4),
        name="solve",
    )(place, weights, primaries, *arrived, *before)


def spread_kernel(sums_ref, *refs):
    out_ref = refs[-1]
    out_ref[...] = jnp.broadcast_to(sums_ref[...][None], out_ref.shape)


def spread(sums, count, after):
    anywhere = pl.BlockSpec(memory_space=pl.ANY)
    vmem = pl.BlockSpec(memory_space=pltpu.VMEM)
    return pl.pallas_call(
        spread_kernel,
        in_specs=[vmem] + [anywhere] * len(after),
        out_specs=vmem,
        out_shape=jax.ShapeDtypeStruct((count,) + sums.shape, F32),
        compiler_params=params(),
        cost_estimate=cost(0, 4 * (count + 1) * sums.size),
        name="spread",
    )(sums, *after)


def update_kernel(sums_ref, resid_ref, pred_ref, out_ref):
    total = jnp.sum(sums_ref[...], axis=0)
    step = jnp.sum(total[0], keepdims=True) / jnp.sum(total[1], keepdims=True)
    out_ref[...] = resid_ref[...] - step[None, None] * pred_ref[...]


def update(sums, resid, pred):
    count, _, n, m = resid.shape
    rows = pl.BlockSpec((1, 2, n, m), lambda i: (i, 0, 0, 0))
    return pl.pallas_call(
        update_kernel,
        grid=(count,),
        in_specs=[pl.BlockSpec(sums.shape, lambda i: (0, 0, 0, 0)), rows, rows],
        out_specs=rows,
        out_shape=jax.ShapeDtypeStruct(resid.shape, F32),
        compiler_params=params(),
        cost_estimate=cost(2 * resid.size, 12 * resid.size),
        name="update",
    )(sums, resid, pred)


def by_offset(values, n_src, n_rcv):
    bits = n_rcv.bit_length() - 1
    rcv = lax.axis_index("rcv")
    values = values.reshape((n_src,) + (2,) * bits + (-1,))
    for axis in range(bits):
        bit = (rcv >> (bits - 1 - axis)) & 1
        values = jnp.where(bit == 1, jnp.flip(values, axis + 1), values)
    return values.reshape(n_src, n_rcv // 2, 2, -1)


def fence(*arrays):
    return lax.optimization_barrier(arrays)


def chunks_of(freq_local):
    edges = [k * freq_local // 4 for k in range(5)]
    return list(zip(edges[:-1], edges[1:]))


def paired_step(traces, freq_index, primaries):
    src_local, rcv_local, samples = traces.shape
    n_src, n_rcv = lax.axis_size("src"), lax.axis_size("rcv")
    n_z = n_rcv // 2
    freq_local = primaries.shape[0]
    src, rcv = lax.axis_index("src"), lax.axis_index("rcv")
    z, core = rcv // 2, rcv % 2
    place = jnp.stack([src, z]).astype(jnp.int32)
    core_id = core.reshape(1).astype(jnp.int32)

    def along(x, offset):
        return lax.ppermute(x, "rcv", [(i, i ^ offset) for i in range(n_rcv)])

    def along_src(x):
        return lax.all_to_all(x, "src", split_axis=0, concat_axis=0, tiled=True)

    def along_z(blocks):
        return [blocks[0]] + [along(blocks[b], 2 * b) for b in range(1, n_z)]

    chunks = chunks_of(freq_local)
    freqs = by_offset(freq_index, n_src, n_rcv)
    freqs = jnp.transpose(freqs, (2, 0, 1, 3))

    def transformed(groups, after=(), swap=True):
        rows = jnp.concatenate([freqs[..., a:b].reshape(-1) for a, b in groups])
        sizes = [n_src * n_z * (b - a) for a, b in groups for _ in range(2)]
        outs = transform(rows, traces, sizes, after)
        outs = [x.reshape(n_src, n_z, -1, src_local, LANES) for x in outs]
        pairs = [(outs[2 * i], outs[2 * i + 1]) for i in range(len(groups))]
        return [(own, along(away, 1) if swap else away) for own, away in pairs]

    weights = freq_index.astype(jnp.float32) / (samples // 2)
    weights = lax.dynamic_slice_in_dim(weights, (src * n_rcv + rcv) * freq_local, freq_local)

    a, b, c, d = chunks
    size = [stop - start for start, stop in chunks]
    a1, a2 = (a[0], a[0] + size[0] // 2), (a[0] + size[0] // 2, a[1])
    half_d = size[3] // 2
    spec_a1, spec_b, spec_a2, spec_c = transformed([a1, b, a2, c])
    first_a1 = merge(core_id, *spec_a1, 0, a1[1] - a1[0], False)
    sent_b = merge(core_id, *spec_b, 0, size[1], True, (first_a1[0],))[0]
    *first_a1, sent_b = fence(*first_a1, sent_b)

    raw_a1 = along_z(first_a1)
    arrived_b = along_src(sent_b)
    first_a2 = merge(core_id, *spec_a2, 0, a2[1] - a2[0], False, (sent_b,))
    sent_c = merge(core_id, *spec_c, 0, size[2], True, (sent_b,))[0]
    (spec_d,) = transformed([d], (sent_b,), False)
    *all_a, arrived_b, sent_c, own_d, away_d, p, q, r, t = fence(
        *raw_a1, arrived_b, sent_c, *spec_d, *first_a2
    )

    raw_a2 = along_z([p, q, r, t])
    arrived_c = along_src(sent_c)
    swapped = along(beside(place, arrived_b), 2)
    packed = pack(place, arrived_b, 0, size[1])
    sent_d = merge(core_id, own_d, along(away_d, 1), 0, size[3], True)[0]
    *all_a, arrived_b, arrived_c, sent_d, swapped, p, q, r = fence(
        *all_a, *raw_a2, arrived_b, arrived_c, sent_d, swapped, *packed
    )

    here_b = along_z([arrived_b] + add_beside(place, arrived_b, swapped, (p, q, r), 0))
    arrived_d = along_src(sent_d)
    swapped = along(beside(place, arrived_c), 2)
    packed = pack(place, arrived_c, 0, size[2])
    whole_a = regroup(all_a[:n_z], all_a[n_z:])
    *here_b, arrived_c, arrived_d, whole_a, swapped, p, q, r = fence(
        *here_b, arrived_c, arrived_d, whole_a, swapped, *packed
    )

    here_c = along_z([arrived_c] + add_beside(place, arrived_c, swapped, (p, q, r), 0))
    whole_a = along_src(whole_a)
    swapped = along(beside(place, arrived_d), 2)
    packed = pack(place, arrived_d, 0, half_d) + pack(place, arrived_d, half_d, size[3] - half_d)
    before = solve(place, weights, primaries, here_b, b[0], ())
    *here_c, arrived_d, whole_a, swapped, p, q, r, t, u, v, x, y, w = fence(
        *here_c, arrived_d, whole_a, swapped, *packed, *before
    )

    here_d = along_z([arrived_d] + add_beside(place, arrived_d, swapped, (p, q, r), 0))
    packed = add_beside(place, arrived_d, swapped, (t, u, v), half_d)
    before = solve(place, weights, primaries, [whole_a], a[0], (x, y, w))
    *here_d, p, q, r, x, y, w = fence(*here_d, *packed, *before)

    last_d = along_z([here_d[0], p, q, r])
    before = solve(place, weights, primaries, here_c, c[0], (x, y, w))
    before = solve(place, weights, primaries, here_d, d[0], before)
    *last_d, x, y, w = fence(*last_d, *before)
    before = solve(place, weights, primaries, last_d, d[0] + half_d, (x, y, w), half_d)

    resid, pred, sums = before
    sums = spread(sums, n_src * n_rcv, (resid, pred))
    sums = lax.all_to_all(sums, AXES, split_axis=0, concat_axis=0, tiled=True)
    return (resid, update(sums, resid, pred))


def solution(mesh):
    in_specs = (P("src", "rcv", None), P(), P(("src", "rcv"), None, None, None))
    out_specs = (P(("src", "rcv"), None, None, None), P(("src", "rcv"), None, None, None))
    n_src, n_rcv = mesh.shape["src"], mesh.shape["rcv"]

    def step(traces, freq_index, primaries):
        src_local, rcv_local, _ = traces.shape
        square = src_local == LANES and 2 * rcv_local == LANES
        if square and n_src == 4 and n_rcv == 2 * n_src and primaries.shape[0] >= 8:
            return paired_step(traces, freq_index, primaries)
        return plain_step(traces, freq_index, primaries)

    return jax.shard_map(step, mesh=mesh, in_specs=in_specs, out_specs=out_specs, check_vma=False)
```

```python
import functools
import math

import jax
import jax.numpy as jnp
from jax import lax
from jax.experimental import pallas as pl
from jax.experimental.pallas import tpu as pltpu
from jax.sharding import PartitionSpec as P

AXES = ("src", "rcv")
LANES = 128
COST_SCALE = 100
VMEM_BYTES = 56 * 1024 * 1024
SMALL_VMEM_BYTES = 14 * 1024 * 1024
F32 = jnp.float32
BF16 = jnp.bfloat16


def freq_table(freq_index, samples):
    times = jnp.arange(samples, dtype=jnp.int32)
    phase = freq_index[:, None] * times[None, :] % samples
    angle = phase.astype(jnp.float32) * (2.0 * math.pi / samples)
    return jnp.stack([jnp.cos(angle), -jnp.sin(angle)], axis=1) / math.sqrt(samples)


def matrix_product(left, right):
    return jnp.einsum("fij,fjk->fik", left, right, precision=lax.Precision.HIGHEST)


def complex_product(left_re, left_im, right_re, right_im, adjoint):
    if adjoint:
        right_re = jnp.swapaxes(right_re, 1, 2)
        right_im = -jnp.swapaxes(right_im, 1, 2)
    real_part = matrix_product(left_re, right_re) - matrix_product(left_im, right_im)
    imag_part = matrix_product(left_re, right_im) + matrix_product(left_im, right_re)
    return (real_part, imag_part)


def plain_step(traces, freq_index, primaries):
    src_local, rcv_local, samples = traces.shape
    n_src = lax.axis_size("src")
    n_rcv = lax.axis_size("rcv")
    table = freq_table(freq_index, samples)
    flat = traces.reshape(src_local * rcv_local, samples)
    spectrum = lax.dot_general(
        table,
        flat,
        (((2,), (1,)), ((), ())),
        precision=lax.Precision.HIGHEST,
        preferred_element_type=jnp.float32,
    )
    spectrum = spectrum[None]
    freq_local = primaries.shape[0]
    arrived = lax.all_to_all(spectrum, AXES, split_axis=1, concat_axis=0, tiled=True)
    arrived = arrived.reshape(n_src, n_rcv, freq_local, 2, src_local, rcv_local)
    arrived = jnp.transpose(arrived, (2, 3, 0, 4, 1, 5))
    whole = arrived.reshape(freq_local, 2, n_src * src_local, n_rcv * rcv_local)
    data_re = 0.5 * (whole[:, 0] + jnp.swapaxes(whole[:, 0], 1, 2))
    data_im = 0.5 * (whole[:, 1] + jnp.swapaxes(whole[:, 1], 1, 2))
    model_re, model_im = complex_product(primaries[:, 0], primaries[:, 1], data_re, data_im, False)
    resid_re = data_re - model_re
    resid_im = data_im - model_im
    grad_re, grad_im = complex_product(resid_re, resid_im, data_re, data_im, True)
    pred_re, pred_im = complex_product(grad_re, grad_im, data_re, data_im, False)
    offset = (lax.axis_index("src") * n_rcv + lax.axis_index("rcv")) * freq_local
    weights = freq_index.astype(jnp.float32) / (samples // 2)
    weights = lax.dynamic_slice_in_dim(weights, offset, freq_local)
    scaled = weights[:, None, None]
    numer = jnp.sum(scaled * (resid_re * pred_re + resid_im * pred_im))
    denom = jnp.sum(scaled * (pred_re * pred_re + pred_im * pred_im))
    numer, denom = lax.psum((numer, denom), AXES)
    step_size = numer / denom
    resid = jnp.stack([resid_re, resid_im], 1)
    pred = jnp.stack([pred_re, pred_im], 1)
    return (resid, resid - step_size * pred)


def params(vmem_bytes=VMEM_BYTES):
    return pltpu.CompilerParams(vmem_limit_bytes=vmem_bytes)


def cost(flops, moved):
    return pl.CostEstimate(flops=int(flops) // COST_SCALE, bytes_accessed=int(moved) // COST_SCALE, transcendentals=0)


def halves(x):
    high = x.astype(BF16)
    return high, (x - high.astype(F32)).astype(BF16)


def product(left, right):
    dot = functools.partial(jnp.dot, preferred_element_type=F32)
    return dot(left[0], right[0]) + (dot(left[0], right[1]) + dot(left[1], right[0]))


def fill_table(table_ref, freq_ref, samples):
    count = freq_ref.shape[0]
    freq = freq_ref[...]
    lane = lax.broadcasted_iota(jnp.int32, (count, LANES), 1)

    def turn(phase):
        angle = (phase & (samples - 1)).astype(F32) * (2.0 * math.pi / samples)
        return jnp.cos(angle), jnp.sin(angle)

    fine_cos, fine_sin = turn(freq * lane)
    coarse_cos, coarse_sin = turn(freq * (lane * LANES))
    scale = 1.0 / math.sqrt(samples)
    for a in range(samples // 2 // LANES):
        cos_a, sin_a = coarse_cos[:, a : a + 1] * scale, coarse_sin[:, a : a + 1] * scale
        cols = slice(a * LANES, (a + 1) * LANES)
        re = halves(cos_a * fine_cos - sin_a * fine_sin)
        im = halves(-(sin_a * fine_cos + cos_a * fine_sin))
        for half in range(2):
            table_ref[0, half * count : (half + 1) * count, cols] = re[half]
            table_ref[1, half * count : (half + 1) * count, cols] = im[half]


def folded(x):
    blocks = x.shape[1] // LANES
    lane = lax.broadcasted_iota(jnp.int32, (x.shape[0], LANES), 1)
    back = (LANES - lane) & (LANES - 1)
    parts = [x[:, a * LANES : (a + 1) * LANES] for a in range(blocks)]
    even, odd = [], []
    for a in range(blocks // 2):
        mirror = jnp.take_along_axis(parts[blocks - 1 - a], back, axis=1, mode="promise_in_bounds")
        first = 0.0 if a == 0 else parts[blocks - a]
        mirror = jnp.where(lane == 0, first, mirror)
        even.append(parts[a] + mirror)
        odd.append(parts[a] - mirror)
    middle = parts[blocks // 2].T[:1]
    return jnp.concatenate(even, axis=1), jnp.concatenate(odd, axis=1), middle


def transform_kernel(splits, freq_ref, traces_ref, *refs):
    out_refs, table_ref = refs[-len(splits) - 1 : -1], refs[-1]
    rows, width, samples = traces_ref.shape
    count = freq_ref.shape[0]

    @pl.when(pl.program_id(0) == 0)
    def _():
        fill_table(table_ref, freq_ref, samples)

    is_left = lax.broadcasted_iota(jnp.int32, (1, LANES), 1) < width
    contract = (((1,), (1,)), ((), ()))
    x = traces_ref[...].reshape(rows * width, samples)
    even, odd, middle = folded(x)
    sums = []
    for part, values in enumerate((even, odd)):
        high, low = halves(values)
        first = lax.dot_general(table_ref[part], high, contract, preferred_element_type=F32)
        second = lax.dot_general(table_ref[part, :count], low, contract, preferred_element_type=F32)
        sums.append(first[:count] + first[count:] + second)
    at_middle = (1 - 2 * (freq_ref[...] & 1)).astype(F32) * (1.0 / math.sqrt(samples))
    sums[0] = sums[0] + at_middle * middle
    for group in range(rows // 8):
        slabs = []
        for pair in range(4 * group, 4 * group + 4):
            cols = slice(pair * LANES, (pair + 1) * LANES)
            re, im = sums[0][:, cols], sums[1][:, cols]
            slabs.append(jnp.where(is_left, re, pltpu.roll(im, width, 1)))
            slabs.append(jnp.where(is_left, pltpu.roll(re, width, 1), im))
        turned = jnp.swapaxes(jnp.stack(slabs, 0), 0, 1)
        for (start, stop), out_ref in zip(splits, out_refs):
            out_ref[:, 8 * group : 8 * group + 8, :] = turned[start:stop]


def transform(freqs, traces, sizes, after=()):
    src_local, rcv_local, samples = traces.shape
    step = min(src_local, 16)
    splits, start = [], 0
    for size in sizes:
        splits.append((start, start + size))
        start += size
    return pl.pallas_call(
        functools.partial(transform_kernel, tuple(splits)),
        grid=(src_local // step,),
        in_specs=[
            pl.BlockSpec((start, 1), lambda i: (0, 0)),
            pl.BlockSpec((step, rcv_local, samples), lambda i: (i, 0, 0)),
        ]
        + [pl.BlockSpec(memory_space=pl.ANY)] * len(after),
        out_specs=[pl.BlockSpec((size, step, LANES), lambda i: (0, i, 0)) for size in sizes],
        out_shape=[jax.ShapeDtypeStruct((size, src_local, LANES), F32) for size in sizes],
        scratch_shapes=[pltpu.VMEM((2, 2 * start, samples // 2), BF16)],
        compiler_params=params(),
        cost_estimate=cost(
            3 * 2 * start * src_local * rcv_local * samples,
            4 * traces.size + 4 * start * src_local * LANES,
        ),
        name="transform",
    )(freqs.reshape(-1, 1), traces, *after)


def merge_kernel(core_ref, own_ref, other_ref, *refs):
    blocks = own_ref.shape[1]
    out_refs = refs[-1:] if len(refs[-1].shape) == 6 else refs[-blocks:]
    width = LANES // 2
    is_left = lax.broadcasted_iota(jnp.int32, (1, LANES), 1) < width
    is_first = core_ref[0] == 0
    for block in range(blocks):
        out_ref = out_refs[0].at[0, block] if len(out_refs) == 1 else out_refs[block].at[0]
        for item in range(own_ref.shape[2]):
            own, other = own_ref[0, block, item], other_ref[0, block, item]
            left = jnp.where(is_first, own, other)
            right = jnp.where(is_first, other, own)
            out_ref[item, 0] = jnp.where(is_left, left, pltpu.roll(right, width, 1))
            out_ref[item, 1] = jnp.where(is_left, pltpu.roll(left, width, 1), right)


def merge(core, own, other, start, count, by_src, after=()):
    n_src, n_z, _, rows, _ = own.shape
    spec = pl.BlockSpec((1, n_z, count, rows, LANES), lambda i, c: (i, 0, start // count, 0, 0))
    if by_src:
        out_specs = [pl.BlockSpec((1, n_z, count, 2, rows, LANES), lambda i, c: (i, 0, 0, 0, 0, 0))]
        out_shape = [jax.ShapeDtypeStruct((n_src, n_z, count, 2, rows, LANES), F32)]
    else:
        out_specs = [pl.BlockSpec((1, count, 2, rows, LANES), lambda i, c: (i, 0, 0, 0, 0))] * n_z
        out_shape = [jax.ShapeDtypeStruct((n_src, count, 2, rows, LANES), F32)] * n_z
    return pl.pallas_call(
        merge_kernel,
        grid_spec=pltpu.PrefetchScalarGridSpec(
            num_scalar_prefetch=1,
            grid=(n_src,),
            in_specs=[spec, spec] + [pl.BlockSpec(memory_space=pl.ANY)] * len(after),
            out_specs=out_specs,
        ),
        out_shape=out_shape,
        compiler_params=params(SMALL_VMEM_BYTES),
        cost_estimate=cost(0, 4 * 4 * n_src * n_z * count * rows * LANES),
        name="merge",
    )(core, own, other, *after)


def regroup_kernel(*refs):
    out_ref = refs[-1]
    blocks = out_ref.shape[1]
    for b in range(blocks):
        start = 0
        for ref in (refs[b], refs[blocks + b]):
            stop = start + ref.shape[1]
            out_ref[0, b, start:stop] = ref[0]
            start = stop


def regroup(part, other):
    n_src, _, *rest = part[0].shape
    count = part[0].shape[1] + other[0].shape[1]
    spec = lambda x: pl.BlockSpec((1,) + x.shape[1:], lambda i: (i, 0, 0, 0, 0))
    return pl.pallas_call(
        regroup_kernel,
        grid=(n_src,),
        in_specs=[spec(x) for x in (*part, *other)],
        out_specs=pl.BlockSpec((1, len(part), count, *rest), lambda i: (i, 0, 0, 0, 0, 0)),
        out_shape=jax.ShapeDtypeStruct((n_src, len(part), count, *rest), F32),
        compiler_params=params(SMALL_VMEM_BYTES),
        cost_estimate=cost(0, 8 * len(part) * (part[0].size + other[0].size)),
        name="regroup",
    )(*part, *other)


def beside_kernel(place_ref, block_ref, out_ref):
    out_ref[...] = block_ref[0, :, :, 0]


def beside(place, blocks):
    _, n_z, count, _, size, _ = blocks.shape
    return pl.pallas_call(
        beside_kernel,
        grid_spec=pltpu.PrefetchScalarGridSpec(
            num_scalar_prefetch=1,
            grid=(1,),
            in_specs=[
                pl.BlockSpec(
                    (1, n_z // 2, count, 1, size, size),
                    lambda i, s: (jnp.bitwise_xor(s[1], 1), 1, 0, 1 - s[1] % 2, 0, 0),
                )
            ],
            out_specs=pl.BlockSpec((n_z // 2, count, size, size), lambda i, s: (0, 0, 0, 0)),
        ),
        out_shape=jax.ShapeDtypeStruct((n_z // 2, count, size, size), F32),
        compiler_params=params(SMALL_VMEM_BYTES),
        cost_estimate=cost(0, 4 * n_z * count * size * size),
        name="beside",
    )(place, blocks)


def put_diagonal(out_ref, start, re, im):
    size = re.shape[0]
    row = lax.broadcasted_iota(jnp.int32, (size, size), 0)
    col = lax.broadcasted_iota(jnp.int32, (size, size), 1)
    lower, upper = re + re.T, im + im.T
    both = jnp.where(row > col, lower, jnp.where(row < col, upper, re))
    out_ref[0, start : start + size, :] = both
    diagonal = jnp.sum(jnp.where(row == col, im, 0.0), axis=0, keepdims=True)
    out_ref[0, start + size :, :] = jnp.broadcast_to(diagonal, (8, size))


def pack_kernel(place_ref, block_ref, near_ref, *far_refs):
    size = LANES
    z = place_ref[1]
    for k in range(1, 4):
        for part in range(2):
            start = (2 * (k - 1) + part) * size
            near_ref[0, start : start + size, :] = block_ref[jnp.bitwise_xor(z, k), 1, 0, part]
    put_diagonal(near_ref, 6 * size, block_ref[z, 1, 0, 0], block_ref[z, 1, 0, 1])
    other_half = 2 * (1 - z // 2)
    for far, far_ref in enumerate(far_refs):
        for part in range(2):
            for k in range(2):
                start = (2 * part + k) * size
                far_ref[0, start : start + size, :] = block_ref[other_half + k, 2 + far, 0, part]
        put_diagonal(far_ref, 5 * size, block_ref[z, 2 + far, 0, 0], block_ref[z, 2 + far, 0, 1])


def pack(place, blocks, start, count):
    n_src, n_z, _, _, size, _ = blocks.shape
    near, far = 7 * size + 8, 6 * size + 8
    return pl.pallas_call(
        pack_kernel,
        grid_spec=pltpu.PrefetchScalarGridSpec(
            num_scalar_prefetch=1,
            grid=(count,),
            in_specs=[pl.BlockSpec((n_src, n_z, 1, 2, size, size), lambda j, s: (0, 0, start + j, 0, 0, 0))],
            out_specs=[pl.BlockSpec((1, rows, size), lambda j, s: (j, 0, 0)) for rows in (near, far, far)],
        ),
        out_shape=[jax.ShapeDtypeStruct((count, rows, size), F32) for rows in (near, far, far)],
        compiler_params=params(SMALL_VMEM_BYTES),
        cost_estimate=cost(0, 4 * 2 * blocks.size),
        name="pack",
    )(place, blocks)


def add_beside_kernel(place_ref, block_ref, swapped_ref, *refs):
    for far, far_ref in enumerate(refs[-2:]):
        for j in range(far_ref.shape[0]):
            far_ref[j] = block_ref[0, far, j, 0] + swapped_ref[1 - far, j].T


def add_beside(place, blocks, swapped, packed, start):
    size = LANES
    near, *fars = packed
    count = near.shape[0]
    spec = pl.BlockSpec((count, size, size), lambda i, s: (0, 4, 0))
    anywhere = pl.BlockSpec(memory_space=pl.ANY)
    fars = pl.pallas_call(
        add_beside_kernel,
        grid_spec=pltpu.PrefetchScalarGridSpec(
            num_scalar_prefetch=1,
            grid=(1,),
            in_specs=[
                pl.BlockSpec(
                    (1, 2, count, 1, size, size),
                    lambda i, s: (jnp.bitwise_xor(s[1], 1), 1, start // count, s[1] % 2, 0, 0),
                ),
                pl.BlockSpec((2, count, size, size), lambda i, s: (0, start // count, 0, 0)),
                anywhere,
                anywhere,
            ],
            out_specs=[spec, spec],
        ),
        out_shape=[jax.ShapeDtypeStruct(x.shape, F32) for x in fars],
        input_output_aliases={3: 0, 4: 1},
        compiler_params=params(SMALL_VMEM_BYTES),
        cost_estimate=cost(0, 4 * 6 * count * size * size),
        name="add_beside",
    )(place, blocks, swapped, *fars)
    return [near, *fars]


def take_diagonal(u_ref, there, packed_ref, start):
    size = LANES
    row = lax.broadcasted_iota(jnp.int32, (size, size), 0)
    col = lax.broadcasted_iota(jnp.int32, (size, size), 1)
    at = pl.ds(pl.multiple_of(there * size, size), size)
    both = packed_ref[0, start : start + size, :]
    diagonal = packed_ref[0, start + size : start + size + 1, :]
    u_ref[0, there, at, :] = jnp.where(row >= col, both, 0.0)
    u_ref[1, there, at, :] = jnp.where(row < col, both, jnp.where(row == col, diagonal, 0.0))


def place_packed(u_ref, place_ref, own_ref, near_ref, *far_refs):
    size = LANES
    z = place_ref[1]
    for part in range(2):
        for source in range(4):
            u_ref[part, z, source * size : (source + 1) * size, :] = own_ref[source, 0, 0, part]
    there = jnp.bitwise_xor(z, 1)
    for k in range(1, 4):
        at = pl.ds(pl.multiple_of(jnp.bitwise_xor(there, k) * size, size), size)
        for part in range(2):
            start = (2 * (k - 1) + part) * size
            u_ref[part, there, at, :] = near_ref[0, start : start + size, :]
    take_diagonal(u_ref, there, near_ref, 6 * size)
    half = pl.ds(pl.multiple_of((z // 2) * 2 * size, size), 2 * size)
    for far, far_ref in enumerate(far_refs):
        there = jnp.bitwise_xor(z, 2 + far)
        for part in range(2):
            u_ref[part, there, half, :] = far_ref[0, 2 * part * size : 2 * (part + 1) * size, :]
        at = pl.ds(pl.multiple_of(jnp.bitwise_xor(there, 1) * size, size), size)
        summed = far_ref[0, 4 * size : 5 * size, :]
        is_re = there % 2 == 0
        u_ref[0, there, at, :] = jnp.where(is_re, summed, 0.0)
        u_ref[1, there, at, :] = jnp.where(is_re, 0.0, summed)
        take_diagonal(u_ref, there, far_ref, 5 * size)


def solve_one(u_ref, data_ref, weight, primaries_ref, resid_ref, pred_ref, sums_ref, is_first, before_ref):
    size = LANES
    blocks = u_ref.shape[1]
    for part in range(2):
        for i in range(blocks):
            for k in range(i, blocks):
                here = slice(i * size, (i + 1) * size)
                there = slice(k * size, (k + 1) * size)
                block = 0.5 * (u_ref[part, k, here, :] + u_ref[part, i, there, :].T)
                data_ref[part, here, there] = block
                if k > i:
                    data_ref[part, there, here] = block.T
    data_re, data_im = data_ref[0], data_ref[1]
    re, im, both = halves(data_re), halves(data_im), halves(data_re + data_im)
    prim_re, prim_im = primaries_ref[0, 0], primaries_ref[0, 1]
    first = product(halves(prim_re), re)
    second = product(halves(prim_im), im)
    third = product(halves(prim_re + prim_im), both)
    resid_re = data_re - (first - second)
    resid_im = data_im - (third - first - second)
    resid_ref[0, 0] = resid_re
    resid_ref[0, 1] = resid_im
    cross = product(re, im)
    turned = cross.T
    gram_re = product(both, both) - (cross + turned)
    gram_im = cross - turned
    first = product(halves(resid_re), halves(gram_re))
    second = product(halves(resid_im), halves(gram_im))
    third = product(halves(resid_re + resid_im), halves(gram_re + gram_im))
    pred_re = first - second
    pred_im = third - first - second
    pred_ref[0, 0] = pred_re
    pred_ref[0, 1] = pred_im

    def fold(x):
        x = x.reshape(x.shape[0] // 8, 8, x.shape[1]).sum(0)
        return sum(x[:, k * LANES : (k + 1) * LANES] for k in range(x.shape[1] // LANES))

    numer = weight * fold(resid_re * pred_re + resid_im * pred_im)
    denom = weight * fold(pred_re * pred_re + pred_im * pred_im)

    @pl.when(is_first)
    def _():
        sums_ref[...] = jnp.zeros_like(sums_ref) if before_ref is None else before_ref[...]

    sums_ref[0] += numer
    sums_ref[1] += denom


def place_raw(u_ref, place_ref, block_ref):
    size = LANES
    z = place_ref[1]
    for source in range(block_ref.shape[0]):
        for b in range(block_ref.shape[1]):
            for part in range(2):
                rows = slice(source * size, (source + 1) * size)
                u_ref[part, jnp.bitwise_xor(z, b), rows, :] = block_ref[source, b, 0, part]


def solve_kernel(offset, n_arrived, n_before, place_ref, weight_ref, primaries_ref, *refs):
    before_ref = refs[n_arrived + 2] if n_before else None
    resid_ref, pred_ref, sums_ref, u_ref, data_ref = refs[-5:]
    j = pl.program_id(0)
    if n_arrived == 1:
        place_raw(u_ref, place_ref, refs[0])
    else:
        place_packed(u_ref, place_ref, *refs[:n_arrived])
    solve_one(u_ref, data_ref, weight_ref[offset + j], primaries_ref, resid_ref, pred_ref, sums_ref, j == 0, before_ref)


def solve(place, weights, primaries, arrived, offset, before, start=0):
    size = LANES
    _, _, n, m = primaries.shape
    n_src, n_z = arrived[0].shape[:2]
    count = arrived[-1].shape[2 if len(arrived) == 1 else 0]
    freq = pl.BlockSpec((1, 2, n, m), lambda j, s: (offset + j, 0, 0, 0))
    if len(arrived) == 1:
        specs = [pl.BlockSpec((n_src, n_z, 1, 2, size, size), lambda j, s: (0, 0, j, 0, 0, 0))]
    else:
        specs = [pl.BlockSpec((n_src, 1, 1, 2, size, size), lambda j, s: (0, 0, start + j, 0, 0, 0))]
        specs += [pl.BlockSpec((1,) + x.shape[1:], lambda j, s: (j, 0, 0)) for x in arrived[1:]]
    sums = pl.BlockSpec((2, 8, LANES), lambda j, s: (0, 0, 0))
    n_before = len(before)
    anywhere = pl.BlockSpec(memory_space=pl.ANY)
    at = 3 + len(specs)
    return pl.pallas_call(
        functools.partial(solve_kernel, offset, len(specs), n_before),
        grid_spec=pltpu.PrefetchScalarGridSpec(
            num_scalar_prefetch=1,
            grid=(count,),
            in_specs=[pl.BlockSpec(memory_space=pltpu.SMEM), freq]
            + specs
            + ([anywhere, anywhere, sums] if n_before else []),
            out_specs=[freq, freq, sums],
            scratch_shapes=[
                pltpu.VMEM((2, n // size, n, size), F32),
                pltpu.VMEM((2, n, m), F32),
            ],
        ),
        out_shape=[
            jax.ShapeDtypeStruct(primaries.shape, F32),
            jax.ShapeDtypeStruct(primaries.shape, F32),
            jax.ShapeDtypeStruct((2, 8, LANES), F32),
        ],
        input_output_aliases={at: 0, at + 1: 1} if n_before else {},
        compiler_params=params(),
        cost_estimate=cost(count * 24 * 2 * n * n * m, count * 4 * 2 * n * m * 4),
        name="solve",
    )(place, weights, primaries, *arrived, *before)


def update_kernel(sums_ref, resid_ref, pred_ref, out_ref):
    total = jnp.sum(sums_ref[...], axis=0)
    step = jnp.sum(total[0], keepdims=True) / jnp.sum(total[1], keepdims=True)
    out_ref[...] = resid_ref[...] - step[None, None] * pred_ref[...]


def update(sums, resid, pred):
    count, _, n, m = resid.shape
    rows = pl.BlockSpec((1, 2, n, m), lambda i: (i, 0, 0, 0))
    return pl.pallas_call(
        update_kernel,
        grid=(count,),
        in_specs=[pl.BlockSpec(sums.shape, lambda i: (0, 0, 0, 0)), rows, rows],
        out_specs=rows,
        out_shape=jax.ShapeDtypeStruct(resid.shape, F32),
        compiler_params=params(),
        cost_estimate=cost(2 * resid.size, 12 * resid.size),
        name="update",
    )(sums, resid, pred)


def by_offset(values, n_src, n_rcv):
    bits = n_rcv.bit_length() - 1
    rcv = lax.axis_index("rcv")
    values = values.reshape((n_src,) + (2,) * bits + (-1,))
    for axis in range(bits):
        bit = (rcv >> (bits - 1 - axis)) & 1
        values = jnp.where(bit == 1, jnp.flip(values, axis + 1), values)
    return values.reshape(n_src, n_rcv // 2, 2, -1)


def fence(*arrays):
    return lax.optimization_barrier(arrays)


def chunks_of(freq_local):
    edges = [k * freq_local // 4 for k in range(5)]
    return list(zip(edges[:-1], edges[1:]))


def paired_step(traces, freq_index, primaries):
    src_local, rcv_local, samples = traces.shape
    n_src, n_rcv = lax.axis_size("src"), lax.axis_size("rcv")
    n_z = n_rcv // 2
    freq_local = primaries.shape[0]
    src, rcv = lax.axis_index("src"), lax.axis_index("rcv")
    z, core = rcv // 2, rcv % 2
    place = jnp.stack([src, z]).astype(jnp.int32)
    core_id = core.reshape(1).astype(jnp.int32)

    def along(x, offset):
        return lax.ppermute(x, "rcv", [(i, i ^ offset) for i in range(n_rcv)])

    def along_src(x):
        return lax.all_to_all(x, "src", split_axis=0, concat_axis=0, tiled=True)

    def along_z(blocks):
        return [blocks[0]] + [along(blocks[b], 2 * b) for b in range(1, n_z)]

    chunks = chunks_of(freq_local)
    freqs = by_offset(freq_index, n_src, n_rcv)
    freqs = jnp.transpose(freqs, (2, 0, 1, 3))

    def transformed(groups, after=(), swap=True):
        rows = jnp.concatenate([freqs[..., a:b].reshape(-1) for a, b in groups])
        sizes = [n_src * n_z * (b - a) for a, b in groups for _ in range(2)]
        outs = transform(rows, traces, sizes, after)
        outs = [x.reshape(n_src, n_z, -1, src_local, LANES) for x in outs]
        pairs = [(outs[2 * i], outs[2 * i + 1]) for i in range(len(groups))]
        return [(own, along(away, 1) if swap else away) for own, away in pairs]

    weights = freq_index.astype(jnp.float32) / (samples // 2)
    weights = lax.dynamic_slice_in_dim(weights, (src * n_rcv + rcv) * freq_local, freq_local)

    a, b, c, d = chunks
    size = [stop - start for start, stop in chunks]
    a1, a2 = (a[0], a[0] + size[0] // 2), (a[0] + size[0] // 2, a[1])
    half_d = size[3] // 2
    spec_a1, spec_b, spec_a2, spec_c = transformed([a1, b, a2, c])
    first_a1 = merge(core_id, *spec_a1, 0, a1[1] - a1[0], False)
    sent_b = merge(core_id, *spec_b, 0, size[1], True, (first_a1[0],))[0]
    *first_a1, sent_b = fence(*first_a1, sent_b)

    raw_a1 = along_z(first_a1)
    arrived_b = along_src(sent_b)
    first_a2 = merge(core_id, *spec_a2, 0, a2[1] - a2[0], False, (sent_b,))
    sent_c = merge(core_id, *spec_c, 0, size[2], True, (sent_b,))[0]
    (spec_d,) = transformed([d], (sent_b,), False)
    *all_a, arrived_b, sent_c, own_d, away_d, p, q, r, t = fence(
        *raw_a1, arrived_b, sent_c, *spec_d, *first_a2
    )

    raw_a2 = along_z([p, q, r, t])
    arrived_c = along_src(sent_c)
    swapped = along(beside(place, arrived_b), 2)
    packed = pack(place, arrived_b, 0, size[1])
    sent_d = merge(core_id, own_d, along(away_d, 1), 0, size[3], True)[0]
    *all_a, arrived_b, arrived_c, sent_d, swapped, p, q, r = fence(
        *all_a, *raw_a2, arrived_b, arrived_c, sent_d, swapped, *packed
    )

    here_b = along_z([arrived_b] + add_beside(place, arrived_b, swapped, (p, q, r), 0))
    arrived_d = along_src(sent_d)
    swapped = along(beside(place, arrived_c), 2)
    packed = pack(place, arrived_c, 0, size[2])
    whole_a = regroup(all_a[:n_z], all_a[n_z:])
    *here_b, arrived_c, arrived_d, whole_a, swapped, p, q, r = fence(
        *here_b, arrived_c, arrived_d, whole_a, swapped, *packed
    )

    here_c = along_z([arrived_c] + add_beside(place, arrived_c, swapped, (p, q, r), 0))
    whole_a = along_src(whole_a)
    swapped = along(beside(place, arrived_d), 2)
    packed = pack(place, arrived_d, 0, half_d) + pack(place, arrived_d, half_d, size[3] - half_d)
    before = solve(place, weights, primaries, here_b, b[0], ())
    *here_c, arrived_d, whole_a, swapped, p, q, r, t, u, v, x, y, w = fence(
        *here_c, arrived_d, whole_a, swapped, *packed, *before
    )

    here_d = along_z([arrived_d] + add_beside(place, arrived_d, swapped, (p, q, r), 0))
    packed = add_beside(place, arrived_d, swapped, (t, u, v), half_d)
    before = solve(place, weights, primaries, [whole_a], a[0], (x, y, w))
    *here_d, p, q, r, x, y, w = fence(*here_d, *packed, *before)

    last_d = along_z([here_d[0], p, q, r])
    before = solve(place, weights, primaries, here_c, c[0], (x, y, w))
    before = solve(place, weights, primaries, here_d, d[0], before)
    *last_d, x, y, w = fence(*last_d, *before)
    before = solve(place, weights, primaries, last_d, d[0] + half_d, (x, y, w), half_d)

    resid, pred, sums = before
    sums = jnp.broadcast_to(sums[None], (n_src * n_rcv,) + sums.shape)
    sums = lax.all_to_all(sums, AXES, split_axis=0, concat_axis=0, tiled=True)
    return (resid, update(sums, resid, pred))


def solution(mesh):
    in_specs = (P("src", "rcv", None), P(), P(("src", "rcv"), None, None, None))
    out_specs = (P(("src", "rcv"), None, None, None), P(("src", "rcv"), None, None, None))
    n_src, n_rcv = mesh.shape["src"], mesh.shape["rcv"]

    def step(traces, freq_index, primaries):
        src_local, rcv_local, _ = traces.shape
        square = src_local == LANES and 2 * rcv_local == LANES
        if square and n_src == 4 and n_rcv == 2 * n_src and primaries.shape[0] >= 8:
            return paired_step(traces, freq_index, primaries)
        return plain_step(traces, freq_index, primaries)

    return jax.shard_map(step, mesh=mesh, in_specs=in_specs, out_specs=out_specs, check_vma=False)
```

```python
import functools
import math

import jax
import jax.numpy as jnp
from jax import lax
from jax.experimental import pallas as pl
from jax.experimental.pallas import tpu as pltpu
from jax.sharding import PartitionSpec as P

AXES = ("src", "rcv")
LANES = 128
COST_SCALE = 100
VMEM_BYTES = 56 * 1024 * 1024
SMALL_VMEM_BYTES = 14 * 1024 * 1024
F32 = jnp.float32
BF16 = jnp.bfloat16


def freq_table(freq_index, samples):
    times = jnp.arange(samples, dtype=jnp.int32)
    phase = freq_index[:, None] * times[None, :] % samples
    angle = phase.astype(jnp.float32) * (2.0 * math.pi / samples)
    return jnp.stack([jnp.cos(angle), -jnp.sin(angle)], axis=1) / math.sqrt(samples)


def matrix_product(left, right):
    return jnp.einsum("fij,fjk->fik", left, right, precision=lax.Precision.HIGHEST)


def complex_product(left_re, left_im, right_re, right_im, adjoint):
    if adjoint:
        right_re = jnp.swapaxes(right_re, 1, 2)
        right_im = -jnp.swapaxes(right_im, 1, 2)
    real_part = matrix_product(left_re, right_re) - matrix_product(left_im, right_im)
    imag_part = matrix_product(left_re, right_im) + matrix_product(left_im, right_re)
    return (real_part, imag_part)


def plain_step(traces, freq_index, primaries):
    src_local, rcv_local, samples = traces.shape
    n_src = lax.axis_size("src")
    n_rcv = lax.axis_size("rcv")
    table = freq_table(freq_index, samples)
    flat = traces.reshape(src_local * rcv_local, samples)
    spectrum = lax.dot_general(
        table,
        flat,
        (((2,), (1,)), ((), ())),
        precision=lax.Precision.HIGHEST,
        preferred_element_type=jnp.float32,
    )
    spectrum = spectrum[None]
    freq_local = primaries.shape[0]
    arrived = lax.all_to_all(spectrum, AXES, split_axis=1, concat_axis=0, tiled=True)
    arrived = arrived.reshape(n_src, n_rcv, freq_local, 2, src_local, rcv_local)
    arrived = jnp.transpose(arrived, (2, 3, 0, 4, 1, 5))
    whole = arrived.reshape(freq_local, 2, n_src * src_local, n_rcv * rcv_local)
    data_re = 0.5 * (whole[:, 0] + jnp.swapaxes(whole[:, 0], 1, 2))
    data_im = 0.5 * (whole[:, 1] + jnp.swapaxes(whole[:, 1], 1, 2))
    model_re, model_im = complex_product(primaries[:, 0], primaries[:, 1], data_re, data_im, False)
    resid_re = data_re - model_re
    resid_im = data_im - model_im
    grad_re, grad_im = complex_product(resid_re, resid_im, data_re, data_im, True)
    pred_re, pred_im = complex_product(grad_re, grad_im, data_re, data_im, False)
    offset = (lax.axis_index("src") * n_rcv + lax.axis_index("rcv")) * freq_local
    weights = freq_index.astype(jnp.float32) / (samples // 2)
    weights = lax.dynamic_slice_in_dim(weights, offset, freq_local)
    scaled = weights[:, None, None]
    numer = jnp.sum(scaled * (resid_re * pred_re + resid_im * pred_im))
    denom = jnp.sum(scaled * (pred_re * pred_re + pred_im * pred_im))
    numer, denom = lax.psum((numer, denom), AXES)
    step_size = numer / denom
    resid = jnp.stack([resid_re, resid_im], 1)
    pred = jnp.stack([pred_re, pred_im], 1)
    return (resid, resid - step_size * pred)


def params(vmem_bytes=VMEM_BYTES):
    return pltpu.CompilerParams(vmem_limit_bytes=vmem_bytes)


def cost(flops, moved):
    return pl.CostEstimate(flops=int(flops) // COST_SCALE, bytes_accessed=int(moved) // COST_SCALE, transcendentals=0)


def halves(x):
    high = x.astype(BF16)
    return high, (x - high.astype(F32)).astype(BF16)


def product(left, right):
    dot = functools.partial(jnp.dot, preferred_element_type=F32)
    return dot(left[0], right[0]) + (dot(left[0], right[1]) + dot(left[1], right[0]))


def fill_table(table_ref, freq_ref, samples):
    count = freq_ref.shape[0]
    freq = freq_ref[...]
    lane = lax.broadcasted_iota(jnp.int32, (count, LANES), 1)

    def turn(phase):
        angle = (phase & (samples - 1)).astype(F32) * (2.0 * math.pi / samples)
        return jnp.cos(angle), jnp.sin(angle)

    fine_cos, fine_sin = turn(freq * lane)
    coarse_cos, coarse_sin = turn(freq * (lane * LANES))
    scale = 1.0 / math.sqrt(samples)
    for a in range(samples // 2 // LANES):
        cos_a, sin_a = coarse_cos[:, a : a + 1] * scale, coarse_sin[:, a : a + 1] * scale
        cols = slice(a * LANES, (a + 1) * LANES)
        re = halves(cos_a * fine_cos - sin_a * fine_sin)
        im = halves(-(sin_a * fine_cos + cos_a * fine_sin))
        for half in range(2):
            table_ref[0, half * count : (half + 1) * count, cols] = re[half]
            table_ref[1, half * count : (half + 1) * count, cols] = im[half]


def folded(x):
    blocks = x.shape[1] // LANES
    lane = lax.broadcasted_iota(jnp.int32, (x.shape[0], LANES), 1)
    back = (LANES - lane) & (LANES - 1)
    parts = [x[:, a * LANES : (a + 1) * LANES] for a in range(blocks)]
    even, odd = [], []
    for a in range(blocks // 2):
        mirror = jnp.take_along_axis(parts[blocks - 1 - a], back, axis=1, mode="promise_in_bounds")
        first = 0.0 if a == 0 else parts[blocks - a]
        mirror = jnp.where(lane == 0, first, mirror)
        even.append(parts[a] + mirror)
        odd.append(parts[a] - mirror)
    middle = parts[blocks // 2].T[:1]
    return jnp.concatenate(even, axis=1), jnp.concatenate(odd, axis=1), middle


def transform_kernel(splits, freq_ref, traces_ref, *refs):
    out_refs, table_ref = refs[-len(splits) - 1 : -1], refs[-1]
    rows, width, samples = traces_ref.shape
    count = freq_ref.shape[0]

    @pl.when(pl.program_id(0) == 0)
    def _():
        fill_table(table_ref, freq_ref, samples)

    is_left = lax.broadcasted_iota(jnp.int32, (1, LANES), 1) < width
    contract = (((1,), (1,)), ((), ()))
    x = traces_ref[...].reshape(rows * width, samples)
    even, odd, middle = folded(x)
    sums = []
    for part, values in enumerate((even, odd)):
        high, low = halves(values)
        first = lax.dot_general(table_ref[part], high, contract, preferred_element_type=F32)
        second = lax.dot_general(table_ref[part, :count], low, contract, preferred_element_type=F32)
        sums.append(first[:count] + first[count:] + second)
    at_middle = (1 - 2 * (freq_ref[...] & 1)).astype(F32) * (1.0 / math.sqrt(samples))
    sums[0] = sums[0] + at_middle * middle
    for group in range(rows // 8):
        slabs = []
        for pair in range(4 * group, 4 * group + 4):
            cols = slice(pair * LANES, (pair + 1) * LANES)
            re, im = sums[0][:, cols], sums[1][:, cols]
            slabs.append(jnp.where(is_left, re, pltpu.roll(im, width, 1)))
            slabs.append(jnp.where(is_left, pltpu.roll(re, width, 1), im))
        turned = jnp.swapaxes(jnp.stack(slabs, 0), 0, 1)
        for (start, stop), out_ref in zip(splits, out_refs):
            out_ref[:, 8 * group : 8 * group + 8, :] = turned[start:stop]


def transform(freqs, traces, sizes, after=()):
    src_local, rcv_local, samples = traces.shape
    step = min(src_local, 16)
    splits, start = [], 0
    for size in sizes:
        splits.append((start, start + size))
        start += size
    return pl.pallas_call(
        functools.partial(transform_kernel, tuple(splits)),
        grid=(src_local // step,),
        in_specs=[
            pl.BlockSpec((start, 1), lambda i: (0, 0)),
            pl.BlockSpec((step, rcv_local, samples), lambda i: (i, 0, 0)),
        ]
        + [pl.BlockSpec(memory_space=pl.ANY)] * len(after),
        out_specs=[pl.BlockSpec((size, step, LANES), lambda i: (0, i, 0)) for size in sizes],
        out_shape=[jax.ShapeDtypeStruct((size, src_local, LANES), F32) for size in sizes],
        scratch_shapes=[pltpu.VMEM((2, 2 * start, samples // 2), BF16)],
        compiler_params=params(),
        cost_estimate=cost(
            3 * 2 * start * src_local * rcv_local * samples,
            4 * traces.size + 4 * start * src_local * LANES,
        ),
        name="transform",
    )(freqs.reshape(-1, 1), traces, *after)


def merge_kernel(core_ref, own_ref, other_ref, *refs):
    blocks = own_ref.shape[1]
    out_refs = refs[-1:] if len(refs[-1].shape) == 6 else refs[-blocks:]
    width = LANES // 2
    is_left = lax.broadcasted_iota(jnp.int32, (1, LANES), 1) < width
    is_first = core_ref[0] == 0
    for block in range(blocks):
        out_ref = out_refs[0].at[0, block] if len(out_refs) == 1 else out_refs[block].at[0]
        for item in range(own_ref.shape[2]):
            own, other = own_ref[0, block, item], other_ref[0, block, item]
            left = jnp.where(is_first, own, other)
            right = jnp.where(is_first, other, own)
            out_ref[item, 0] = jnp.where(is_left, left, pltpu.roll(right, width, 1))
            out_ref[item, 1] = jnp.where(is_left, pltpu.roll(left, width, 1), right)


def merge(core, own, other, start, count, by_src, after=()):
    n_src, n_z, _, rows, _ = own.shape
    spec = pl.BlockSpec((1, n_z, count, rows, LANES), lambda i, c: (i, 0, start // count, 0, 0))
    if by_src:
        out_specs = [pl.BlockSpec((1, n_z, count, 2, rows, LANES), lambda i, c: (i, 0, 0, 0, 0, 0))]
        out_shape = [jax.ShapeDtypeStruct((n_src, n_z, count, 2, rows, LANES), F32)]
    else:
        out_specs = [pl.BlockSpec((1, count, 2, rows, LANES), lambda i, c: (i, 0, 0, 0, 0))] * n_z
        out_shape = [jax.ShapeDtypeStruct((n_src, count, 2, rows, LANES), F32)] * n_z
    return pl.pallas_call(
        merge_kernel,
        grid_spec=pltpu.PrefetchScalarGridSpec(
            num_scalar_prefetch=1,
            grid=(n_src,),
            in_specs=[spec, spec] + [pl.BlockSpec(memory_space=pl.ANY)] * len(after),
            out_specs=out_specs,
        ),
        out_shape=out_shape,
        compiler_params=params(SMALL_VMEM_BYTES),
        cost_estimate=cost(0, 4 * 4 * n_src * n_z * count * rows * LANES),
        name="merge",
    )(core, own, other, *after)


def regroup_kernel(*refs):
    out_ref = refs[-1]
    blocks = out_ref.shape[1]
    for b in range(blocks):
        start = 0
        for ref in (refs[b], refs[blocks + b]):
            stop = start + ref.shape[1]
            out_ref[0, b, start:stop] = ref[0]
            start = stop


def regroup(part, other):
    n_src, _, *rest = part[0].shape
    count = part[0].shape[1] + other[0].shape[1]
    spec = lambda x: pl.BlockSpec((1,) + x.shape[1:], lambda i: (i, 0, 0, 0, 0))
    return pl.pallas_call(
        regroup_kernel,
        grid=(n_src,),
        in_specs=[spec(x) for x in (*part, *other)],
        out_specs=pl.BlockSpec((1, len(part), count, *rest), lambda i: (i, 0, 0, 0, 0, 0)),
        out_shape=jax.ShapeDtypeStruct((n_src, len(part), count, *rest), F32),
        compiler_params=params(SMALL_VMEM_BYTES),
        cost_estimate=cost(0, 8 * len(part) * (part[0].size + other[0].size)),
        name="regroup",
    )(*part, *other)


def beside_kernel(place_ref, block_ref, out_ref):
    out_ref[...] = block_ref[0, :, :, 0]


def beside(place, blocks):
    _, n_z, count, _, size, _ = blocks.shape
    return pl.pallas_call(
        beside_kernel,
        grid_spec=pltpu.PrefetchScalarGridSpec(
            num_scalar_prefetch=1,
            grid=(1,),
            in_specs=[
                pl.BlockSpec(
                    (1, n_z // 2, count, 1, size, size),
                    lambda i, s: (jnp.bitwise_xor(s[1], 1), 1, 0, 1 - s[1] % 2, 0, 0),
                )
            ],
            out_specs=pl.BlockSpec((n_z // 2, count, size, size), lambda i, s: (0, 0, 0, 0)),
        ),
        out_shape=jax.ShapeDtypeStruct((n_z // 2, count, size, size), F32),
        compiler_params=params(SMALL_VMEM_BYTES),
        cost_estimate=cost(0, 4 * n_z * count * size * size),
        name="beside",
    )(place, blocks)


def put_diagonal(out_ref, start, re, im):
    size = re.shape[0]
    row = lax.broadcasted_iota(jnp.int32, (size, size), 0)
    col = lax.broadcasted_iota(jnp.int32, (size, size), 1)
    lower, upper = re + re.T, im + im.T
    both = jnp.where(row > col, lower, jnp.where(row < col, upper, re))
    out_ref[0, start : start + size, :] = both
    diagonal = jnp.sum(jnp.where(row == col, im, 0.0), axis=0, keepdims=True)
    out_ref[0, start + size :, :] = jnp.broadcast_to(diagonal, (8, size))


def pack_kernel(place_ref, block_ref, near_ref, *far_refs):
    size = LANES
    z = place_ref[1]
    for k in range(1, 4):
        for part in range(2):
            start = (2 * (k - 1) + part) * size
            near_ref[0, start : start + size, :] = block_ref[jnp.bitwise_xor(z, k), 1, 0, part]
    put_diagonal(near_ref, 6 * size, block_ref[z, 1, 0, 0], block_ref[z, 1, 0, 1])
    other_half = 2 * (1 - z // 2)
    for far, far_ref in enumerate(far_refs):
        for part in range(2):
            for k in range(2):
                start = (2 * part + k) * size
                far_ref[0, start : start + size, :] = block_ref[other_half + k, 2 + far, 0, part]
        put_diagonal(far_ref, 5 * size, block_ref[z, 2 + far, 0, 0], block_ref[z, 2 + far, 0, 1])


def pack(place, blocks, start, count):
    n_src, n_z, _, _, size, _ = blocks.shape
    near, far = 7 * size + 8, 6 * size + 8
    return pl.pallas_call(
        pack_kernel,
        grid_spec=pltpu.PrefetchScalarGridSpec(
            num_scalar_prefetch=1,
            grid=(count,),
            in_specs=[pl.BlockSpec((n_src, n_z, 1, 2, size, size), lambda j, s: (0, 0, start + j, 0, 0, 0))],
            out_specs=[pl.BlockSpec((1, rows, size), lambda j, s: (j, 0, 0)) for rows in (near, far, far)],
        ),
        out_shape=[jax.ShapeDtypeStruct((count, rows, size), F32) for rows in (near, far, far)],
        compiler_params=params(SMALL_VMEM_BYTES),
        cost_estimate=cost(0, 4 * 2 * blocks.size),
        name="pack",
    )(place, blocks)


def add_beside_kernel(place_ref, block_ref, swapped_ref, *refs):
    for far, far_ref in enumerate(refs[-2:]):
        for j in range(far_ref.shape[0]):
            far_ref[j] = block_ref[0, far, j, 0] + swapped_ref[1 - far, j].T


def add_beside(place, blocks, swapped, packed, start):
    size = LANES
    near, *fars = packed
    count = fars[0].shape[0]
    spec = pl.BlockSpec((count, size, size), lambda i, s: (0, 4, 0))
    anywhere = pl.BlockSpec(memory_space=pl.ANY)
    fars = pl.pallas_call(
        add_beside_kernel,
        grid_spec=pltpu.PrefetchScalarGridSpec(
            num_scalar_prefetch=1,
            grid=(1,),
            in_specs=[
                pl.BlockSpec(
                    (1, 2, count, 1, size, size),
                    lambda i, s: (jnp.bitwise_xor(s[1], 1), 1, start // count, s[1] % 2, 0, 0),
                ),
                pl.BlockSpec((2, count, size, size), lambda i, s: (0, start // count, 0, 0)),
                anywhere,
                anywhere,
            ],
            out_specs=[spec, spec],
        ),
        out_shape=[jax.ShapeDtypeStruct(x.shape, F32) for x in fars],
        input_output_aliases={3: 0, 4: 1},
        compiler_params=params(SMALL_VMEM_BYTES),
        cost_estimate=cost(0, 4 * 6 * count * size * size),
        name="add_beside",
    )(place, blocks, swapped, *fars)
    return [near, *fars]


def take_diagonal(u_ref, there, packed_ref, start):
    size = LANES
    row = lax.broadcasted_iota(jnp.int32, (size, size), 0)
    col = lax.broadcasted_iota(jnp.int32, (size, size), 1)
    at = pl.ds(pl.multiple_of(there * size, size), size)
    both = packed_ref[0, start : start + size, :]
    diagonal = packed_ref[0, start + size : start + size + 1, :]
    u_ref[0, there, at, :] = jnp.where(row >= col, both, 0.0)
    u_ref[1, there, at, :] = jnp.where(row < col, both, jnp.where(row == col, diagonal, 0.0))


def place_packed(u_ref, place_ref, own_ref, near_ref, *far_refs):
    size = LANES
    z = place_ref[1]
    for part in range(2):
        for source in range(4):
            u_ref[part, z, source * size : (source + 1) * size, :] = own_ref[source, 0, 0, part]
    there = jnp.bitwise_xor(z, 1)
    for k in range(1, 4):
        at = pl.ds(pl.multiple_of(jnp.bitwise_xor(there, k) * size, size), size)
        for part in range(2):
            start = (2 * (k - 1) + part) * size
            u_ref[part, there, at, :] = near_ref[0, start : start + size, :]
    take_diagonal(u_ref, there, near_ref, 6 * size)
    half = pl.ds(pl.multiple_of((z // 2) * 2 * size, size), 2 * size)
    for far, far_ref in enumerate(far_refs):
        there = jnp.bitwise_xor(z, 2 + far)
        for part in range(2):
            u_ref[part, there, half, :] = far_ref[0, 2 * part * size : 2 * (part + 1) * size, :]
        at = pl.ds(pl.multiple_of(jnp.bitwise_xor(there, 1) * size, size), size)
        summed = far_ref[0, 4 * size : 5 * size, :]
        is_re = there % 2 == 0
        u_ref[0, there, at, :] = jnp.where(is_re, summed, 0.0)
        u_ref[1, there, at, :] = jnp.where(is_re, 0.0, summed)
        take_diagonal(u_ref, there, far_ref, 5 * size)


def solve_one(u_ref, data_ref, weight, primaries_ref, resid_ref, pred_ref, sums_ref, is_first, before_ref):
    size = LANES
    blocks = u_ref.shape[1]
    for part in range(2):
        for i in range(blocks):
            for k in range(i, blocks):
                here = slice(i * size, (i + 1) * size)
                there = slice(k * size, (k + 1) * size)
                block = 0.5 * (u_ref[part, k, here, :] + u_ref[part, i, there, :].T)
                data_ref[part, here, there] = block
                if k > i:
                    data_ref[part, there, here] = block.T
    data_re, data_im = data_ref[0], data_ref[1]
    re, im, both = halves(data_re), halves(data_im), halves(data_re + data_im)
    prim_re, prim_im = primaries_ref[0, 0], primaries_ref[0, 1]
    first = product(halves(prim_re), re)
    second = product(halves(prim_im), im)
    third = product(halves(prim_re + prim_im), both)
    resid_re = data_re - (first - second)
    resid_im = data_im - (third - first - second)
    resid_ref[0, 0] = resid_re
    resid_ref[0, 1] = resid_im
    cross = product(re, im)
    turned = cross.T
    gram_re = product(both, both) - (cross + turned)
    gram_im = cross - turned
    first = product(halves(resid_re), halves(gram_re))
    second = product(halves(resid_im), halves(gram_im))
    third = product(halves(resid_re + resid_im), halves(gram_re + gram_im))
    pred_re = first - second
    pred_im = third - first - second
    pred_ref[0, 0] = pred_re
    pred_ref[0, 1] = pred_im

    def fold(x):
        x = x.reshape(x.shape[0] // 8, 8, x.shape[1]).sum(0)
        return sum(x[:, k * LANES : (k + 1) * LANES] for k in range(x.shape[1] // LANES))

    numer = weight * fold(resid_re * pred_re + resid_im * pred_im)
    denom = weight * fold(pred_re * pred_re + pred_im * pred_im)

    @pl.when(is_first)
    def _():
        sums_ref[...] = jnp.zeros_like(sums_ref) if before_ref is None else before_ref[...]

    sums_ref[0] += numer
    sums_ref[1] += denom


def place_raw(u_ref, place_ref, block_ref):
    size = LANES
    z = place_ref[1]
    for source in range(block_ref.shape[0]):
        for b in range(block_ref.shape[1]):
            for part in range(2):
                rows = slice(source * size, (source + 1) * size)
                u_ref[part, jnp.bitwise_xor(z, b), rows, :] = block_ref[source, b, 0, part]


def solve_kernel(offset, n_arrived, n_before, place_ref, weight_ref, primaries_ref, *refs):
    before_ref = refs[n_arrived + 2] if n_before else None
    resid_ref, pred_ref, sums_ref, u_ref, data_ref = refs[-5:]
    j = pl.program_id(0)
    if n_arrived == 1:
        place_raw(u_ref, place_ref, refs[0])
    else:
        place_packed(u_ref, place_ref, *refs[:n_arrived])
    solve_one(u_ref, data_ref, weight_ref[offset + j], primaries_ref, resid_ref, pred_ref, sums_ref, j == 0, before_ref)


def solve(place, weights, primaries, arrived, offset, before, start=0):
    size = LANES
    _, _, n, m = primaries.shape
    n_src, n_z = arrived[0].shape[:2]
    count = arrived[-1].shape[2 if len(arrived) == 1 else 0]
    freq = pl.BlockSpec((1, 2, n, m), lambda j, s: (offset + j, 0, 0, 0))
    if len(arrived) == 1:
        specs = [pl.BlockSpec((n_src, n_z, 1, 2, size, size), lambda j, s: (0, 0, j, 0, 0, 0))]
    else:
        specs = [pl.BlockSpec((n_src, 1, 1, 2, size, size), lambda j, s: (0, 0, start + j, 0, 0, 0))]
        for x in arrived[1:]:
            base = start if x.shape[0] > count else 0
            specs.append(pl.BlockSpec((1,) + x.shape[1:], lambda j, s, base=base: (base + j, 0, 0)))
    sums = pl.BlockSpec((2, 8, LANES), lambda j, s: (0, 0, 0))
    n_before = len(before)
    anywhere = pl.BlockSpec(memory_space=pl.ANY)
    at = 3 + len(specs)
    return pl.pallas_call(
        functools.partial(solve_kernel, offset, len(specs), n_before),
        grid_spec=pltpu.PrefetchScalarGridSpec(
            num_scalar_prefetch=1,
            grid=(count,),
            in_specs=[pl.BlockSpec(memory_space=pltpu.SMEM), freq]
            + specs
            + ([anywhere, anywhere, sums] if n_before else []),
            out_specs=[freq, freq, sums],
            scratch_shapes=[
                pltpu.VMEM((2, n // size, n, size), F32),
                pltpu.VMEM((2, n, m), F32),
            ],
        ),
        out_shape=[
            jax.ShapeDtypeStruct(primaries.shape, F32),
            jax.ShapeDtypeStruct(primaries.shape, F32),
            jax.ShapeDtypeStruct((2, 8, LANES), F32),
        ],
        input_output_aliases={at: 0, at + 1: 1} if n_before else {},
        compiler_params=params(),
        cost_estimate=cost(count * 24 * 2 * n * n * m, count * 4 * 2 * n * m * 4),
        name="solve",
    )(place, weights, primaries, *arrived, *before)


def update_kernel(sums_ref, resid_ref, pred_ref, out_ref):
    total = jnp.sum(sums_ref[...], axis=0)
    step = jnp.sum(total[0], keepdims=True) / jnp.sum(total[1], keepdims=True)
    out_ref[...] = resid_ref[...] - step[None, None] * pred_ref[...]


def update(sums, resid, pred):
    count, _, n, m = resid.shape
    rows = pl.BlockSpec((1, 2, n, m), lambda i: (i, 0, 0, 0))
    return pl.pallas_call(
        update_kernel,
        grid=(count,),
        in_specs=[pl.BlockSpec(sums.shape, lambda i: (0, 0, 0, 0)), rows, rows],
        out_specs=rows,
        out_shape=jax.ShapeDtypeStruct(resid.shape, F32),
        compiler_params=params(),
        cost_estimate=cost(2 * resid.size, 12 * resid.size),
        name="update",
    )(sums, resid, pred)


def by_offset(values, n_src, n_rcv):
    bits = n_rcv.bit_length() - 1
    rcv = lax.axis_index("rcv")
    values = values.reshape((n_src,) + (2,) * bits + (-1,))
    for axis in range(bits):
        bit = (rcv >> (bits - 1 - axis)) & 1
        values = jnp.where(bit == 1, jnp.flip(values, axis + 1), values)
    return values.reshape(n_src, n_rcv // 2, 2, -1)


def fence(*arrays):
    return lax.optimization_barrier(arrays)


def chunks_of(freq_local):
    edges = [k * freq_local // 4 for k in range(5)]
    return list(zip(edges[:-1], edges[1:]))


def paired_step(traces, freq_index, primaries):
    src_local, rcv_local, samples = traces.shape
    n_src, n_rcv = lax.axis_size("src"), lax.axis_size("rcv")
    n_z = n_rcv // 2
    freq_local = primaries.shape[0]
    src, rcv = lax.axis_index("src"), lax.axis_index("rcv")
    z, core = rcv // 2, rcv % 2
    place = jnp.stack([src, z]).astype(jnp.int32)
    core_id = core.reshape(1).astype(jnp.int32)

    def along(x, offset):
        return lax.ppermute(x, "rcv", [(i, i ^ offset) for i in range(n_rcv)])

    def along_src(x):
        return lax.all_to_all(x, "src", split_axis=0, concat_axis=0, tiled=True)

    def along_z(blocks):
        return [blocks[0]] + [along(blocks[b], 2 * b) for b in range(1, n_z)]

    chunks = chunks_of(freq_local)
    freqs = by_offset(freq_index, n_src, n_rcv)
    freqs = jnp.transpose(freqs, (2, 0, 1, 3))

    def transformed(groups, after=(), swap=True):
        rows = jnp.concatenate([freqs[..., a:b].reshape(-1) for a, b in groups])
        sizes = [n_src * n_z * (b - a) for a, b in groups for _ in range(2)]
        outs = transform(rows, traces, sizes, after)
        outs = [x.reshape(n_src, n_z, -1, src_local, LANES) for x in outs]
        pairs = [(outs[2 * i], outs[2 * i + 1]) for i in range(len(groups))]
        return [(own, along(away, 1) if swap else away) for own, away in pairs]

    weights = freq_index.astype(jnp.float32) / (samples // 2)
    weights = lax.dynamic_slice_in_dim(weights, (src * n_rcv + rcv) * freq_local, freq_local)

    a, b, c, d = chunks
    size = [stop - start for start, stop in chunks]
    a1, a2 = (a[0], a[0] + size[0] // 2), (a[0] + size[0] // 2, a[1])
    half_d = size[3] // 2
    spec_a1, spec_b, spec_a2, spec_c = transformed([a1, b, a2, c])
    first_a1 = merge(core_id, *spec_a1, 0, a1[1] - a1[0], False)
    sent_b = merge(core_id, *spec_b, 0, size[1], True, (first_a1[0],))[0]
    *first_a1, sent_b = fence(*first_a1, sent_b)

    raw_a1 = along_z(first_a1)
    arrived_b = along_src(sent_b)
    first_a2 = merge(core_id, *spec_a2, 0, a2[1] - a2[0], False, (sent_b,))
    sent_c = merge(core_id, *spec_c, 0, size[2], True, (sent_b,))[0]
    (spec_d,) = transformed([d], (sent_b,), False)
    *all_a, arrived_b, sent_c, own_d, away_d, p, q, r, t = fence(
        *raw_a1, arrived_b, sent_c, *spec_d, *first_a2
    )

    raw_a2 = along_z([p, q, r, t])
    arrived_c = along_src(sent_c)
    swapped = along(beside(place, arrived_b), 2)
    packed = pack(place, arrived_b, 0, size[1])
    sent_d = merge(core_id, own_d, along(away_d, 1), 0, size[3], True)[0]
    *all_a, arrived_b, arrived_c, sent_d, swapped, p, q, r = fence(
        *all_a, *raw_a2, arrived_b, arrived_c, sent_d, swapped, *packed
    )

    here_b = along_z([arrived_b] + add_beside(place, arrived_b, swapped, (p, q, r), 0))
    arrived_d = along_src(sent_d)
    swapped = along(beside(place, arrived_c), 2)
    packed = pack(place, arrived_c, 0, size[2])
    whole_a = regroup(all_a[:n_z], all_a[n_z:])
    *here_b, arrived_c, arrived_d, whole_a, swapped, p, q, r = fence(
        *here_b, arrived_c, arrived_d, whole_a, swapped, *packed
    )

    here_c = along_z([arrived_c] + add_beside(place, arrived_c, swapped, (p, q, r), 0))
    whole_a = along_src(whole_a)
    swapped = along(beside(place, arrived_d), 2)
    near = pack(place, arrived_d, 0, size[3])[0]
    far_1 = pack(place, arrived_d, 0, half_d)[1:]
    far_2 = pack(place, arrived_d, half_d, size[3] - half_d)[1:]
    packed = [near, *far_1, *far_2]
    before = solve(place, weights, primaries, here_b, b[0], ())
    *here_c, arrived_d, whole_a, swapped, p, q, r, t, u, x, y, w = fence(
        *here_c, arrived_d, whole_a, swapped, *packed, *before
    )

    here_d = along_z([arrived_d] + add_beside(place, arrived_d, swapped, (p, q, r), 0))
    _, *fars = add_beside(place, arrived_d, swapped, (p, t, u), half_d)
    last_d = here_d[:2] + [along(x, 2 * b) for b, x in enumerate(fars, 2)]
    before = solve(place, weights, primaries, [whole_a], a[0], (x, y, w))
    before = solve(place, weights, primaries, here_c, c[0], before)
    before = solve(place, weights, primaries, here_d, d[0], before)
    before = solve(place, weights, primaries, last_d, d[0] + half_d, before, half_d)

    resid, pred, sums = before
    sums = jnp.broadcast_to(sums[None], (n_src * n_rcv,) + sums.shape)
    sums = lax.all_to_all(sums, AXES, split_axis=0, concat_axis=0, tiled=True)
    return (resid, update(sums, resid, pred))


def solution(mesh):
    in_specs = (P("src", "rcv", None), P(), P(("src", "rcv"), None, None, None))
    out_specs = (P(("src", "rcv"), None, None, None), P(("src", "rcv"), None, None, None))
    n_src, n_rcv = mesh.shape["src"], mesh.shape["rcv"]

    def step(traces, freq_index, primaries):
        src_local, rcv_local, _ = traces.shape
        square = src_local == LANES and 2 * rcv_local == LANES
        if square and n_src == 4 and n_rcv == 2 * n_src and primaries.shape[0] >= 8:
            return paired_step(traces, freq_index, primaries)
        return plain_step(traces, freq_index, primaries)

    return jax.shard_map(step, mesh=mesh, in_specs=in_specs, out_specs=out_specs, check_vma=False)
```

```python
import functools
import math

import jax
import jax.numpy as jnp
from jax import lax
from jax.experimental import pallas as pl
from jax.experimental.pallas import tpu as pltpu
from jax.sharding import PartitionSpec as P

AXES = ("src", "rcv")
LANES = 128
COST_SCALE = 100
VMEM_BYTES = 56 * 1024 * 1024
SMALL_VMEM_BYTES = 14 * 1024 * 1024
F32 = jnp.float32
BF16 = jnp.bfloat16


def freq_table(freq_index, samples):
    times = jnp.arange(samples, dtype=jnp.int32)
    phase = freq_index[:, None] * times[None, :] % samples
    angle = phase.astype(jnp.float32) * (2.0 * math.pi / samples)
    return jnp.stack([jnp.cos(angle), -jnp.sin(angle)], axis=1) / math.sqrt(samples)


def matrix_product(left, right):
    return jnp.einsum("fij,fjk->fik", left, right, precision=lax.Precision.HIGHEST)


def complex_product(left_re, left_im, right_re, right_im, adjoint):
    if adjoint:
        right_re = jnp.swapaxes(right_re, 1, 2)
        right_im = -jnp.swapaxes(right_im, 1, 2)
    real_part = matrix_product(left_re, right_re) - matrix_product(left_im, right_im)
    imag_part = matrix_product(left_re, right_im) + matrix_product(left_im, right_re)
    return (real_part, imag_part)


def plain_step(traces, freq_index, primaries):
    src_local, rcv_local, samples = traces.shape
    n_src = lax.axis_size("src")
    n_rcv = lax.axis_size("rcv")
    table = freq_table(freq_index, samples)
    flat = traces.reshape(src_local * rcv_local, samples)
    spectrum = lax.dot_general(
        table,
        flat,
        (((2,), (1,)), ((), ())),
        precision=lax.Precision.HIGHEST,
        preferred_element_type=jnp.float32,
    )
    spectrum = spectrum[None]
    freq_local = primaries.shape[0]
    arrived = lax.all_to_all(spectrum, AXES, split_axis=1, concat_axis=0, tiled=True)
    arrived = arrived.reshape(n_src, n_rcv, freq_local, 2, src_local, rcv_local)
    arrived = jnp.transpose(arrived, (2, 3, 0, 4, 1, 5))
    whole = arrived.reshape(freq_local, 2, n_src * src_local, n_rcv * rcv_local)
    data_re = 0.5 * (whole[:, 0] + jnp.swapaxes(whole[:, 0], 1, 2))
    data_im = 0.5 * (whole[:, 1] + jnp.swapaxes(whole[:, 1], 1, 2))
    model_re, model_im = complex_product(primaries[:, 0], primaries[:, 1], data_re, data_im, False)
    resid_re = data_re - model_re
    resid_im = data_im - model_im
    grad_re, grad_im = complex_product(resid_re, resid_im, data_re, data_im, True)
    pred_re, pred_im = complex_product(grad_re, grad_im, data_re, data_im, False)
    offset = (lax.axis_index("src") * n_rcv + lax.axis_index("rcv")) * freq_local
    weights = freq_index.astype(jnp.float32) / (samples // 2)
    weights = lax.dynamic_slice_in_dim(weights, offset, freq_local)
    scaled = weights[:, None, None]
    numer = jnp.sum(scaled * (resid_re * pred_re + resid_im * pred_im))
    denom = jnp.sum(scaled * (pred_re * pred_re + pred_im * pred_im))
    numer, denom = lax.psum((numer, denom), AXES)
    step_size = numer / denom
    resid = jnp.stack([resid_re, resid_im], 1)
    pred = jnp.stack([pred_re, pred_im], 1)
    return (resid, resid - step_size * pred)


def params(vmem_bytes=VMEM_BYTES):
    return pltpu.CompilerParams(vmem_limit_bytes=vmem_bytes)


def cost(flops, moved):
    return pl.CostEstimate(flops=int(flops) // COST_SCALE, bytes_accessed=int(moved) // COST_SCALE, transcendentals=0)


def halves(x):
    high = x.astype(BF16)
    return high, (x - high.astype(F32)).astype(BF16)


def product(left, right):
    dot = functools.partial(jnp.dot, preferred_element_type=F32)
    return dot(left[0], right[0]) + (dot(left[0], right[1]) + dot(left[1], right[0]))


def fill_table(table_ref, freq_ref, samples):
    count = freq_ref.shape[0]
    freq = freq_ref[...]
    lane = lax.broadcasted_iota(jnp.int32, (count, LANES), 1)

    def turn(phase):
        angle = (phase & (samples - 1)).astype(F32) * (2.0 * math.pi / samples)
        return jnp.cos(angle), jnp.sin(angle)

    fine_cos, fine_sin = turn(freq * lane)
    coarse_cos, coarse_sin = turn(freq * (lane * LANES))
    scale = 1.0 / math.sqrt(samples)
    for a in range(samples // 2 // LANES):
        cos_a, sin_a = coarse_cos[:, a : a + 1] * scale, coarse_sin[:, a : a + 1] * scale
        cols = slice(a * LANES, (a + 1) * LANES)
        re = halves(cos_a * fine_cos - sin_a * fine_sin)
        im = halves(-(sin_a * fine_cos + cos_a * fine_sin))
        for half in range(2):
            table_ref[0, half * count : (half + 1) * count, cols] = re[half]
            table_ref[1, half * count : (half + 1) * count, cols] = im[half]


def folded(x):
    blocks = x.shape[1] // LANES
    lane = lax.broadcasted_iota(jnp.int32, (x.shape[0], LANES), 1)
    back = (LANES - lane) & (LANES - 1)
    parts = [x[:, a * LANES : (a + 1) * LANES] for a in range(blocks)]
    even, odd = [], []
    for a in range(blocks // 2):
        mirror = jnp.take_along_axis(parts[blocks - 1 - a], back, axis=1, mode="promise_in_bounds")
        first = 0.0 if a == 0 else parts[blocks - a]
        mirror = jnp.where(lane == 0, first, mirror)
        even.append(parts[a] + mirror)
        odd.append(parts[a] - mirror)
    middle = parts[blocks // 2].T[:1]
    return jnp.concatenate(even, axis=1), jnp.concatenate(odd, axis=1), middle


def transform_kernel(splits, freq_ref, traces_ref, *refs):
    out_refs, table_ref = refs[-len(splits) - 1 : -1], refs[-1]
    rows, width, samples = traces_ref.shape
    count = freq_ref.shape[0]

    @pl.when(pl.program_id(0) == 0)
    def _():
        fill_table(table_ref, freq_ref, samples)

    is_left = lax.broadcasted_iota(jnp.int32, (1, LANES), 1) < width
    contract = (((1,), (1,)), ((), ()))
    x = traces_ref[...].reshape(rows * width, samples)
    even, odd, middle = folded(x)
    sums = []
    for part, values in enumerate((even, odd)):
        high, low = halves(values)
        first = lax.dot_general(table_ref[part], high, contract, preferred_element_type=F32)
        second = lax.dot_general(table_ref[part, :count], low, contract, preferred_element_type=F32)
        sums.append(first[:count] + first[count:] + second)
    at_middle = (1 - 2 * (freq_ref[...] & 1)).astype(F32) * (1.0 / math.sqrt(samples))
    sums[0] = sums[0] + at_middle * middle
    for group in range(rows // 8):
        slabs = []
        for pair in range(4 * group, 4 * group + 4):
            cols = slice(pair * LANES, (pair + 1) * LANES)
            re, im = sums[0][:, cols], sums[1][:, cols]
            slabs.append(jnp.where(is_left, re, pltpu.roll(im, width, 1)))
            slabs.append(jnp.where(is_left, pltpu.roll(re, width, 1), im))
        turned = jnp.swapaxes(jnp.stack(slabs, 0), 0, 1)
        for (start, stop), out_ref in zip(splits, out_refs):
            out_ref[:, 8 * group : 8 * group + 8, :] = turned[start:stop]


def transform(freqs, traces, sizes, after=()):
    src_local, rcv_local, samples = traces.shape
    step = min(src_local, 32)
    splits, start = [], 0
    for size in sizes:
        splits.append((start, start + size))
        start += size
    return pl.pallas_call(
        functools.partial(transform_kernel, tuple(splits)),
        grid=(src_local // step,),
        in_specs=[
            pl.BlockSpec((start, 1), lambda i: (0, 0)),
            pl.BlockSpec((step, rcv_local, samples), lambda i: (i, 0, 0)),
        ]
        + [pl.BlockSpec(memory_space=pl.ANY)] * len(after),
        out_specs=[pl.BlockSpec((size, step, LANES), lambda i: (0, i, 0)) for size in sizes],
        out_shape=[jax.ShapeDtypeStruct((size, src_local, LANES), F32) for size in sizes],
        scratch_shapes=[pltpu.VMEM((2, 2 * start, samples // 2), BF16)],
        compiler_params=params(),
        cost_estimate=cost(
            3 * 2 * start * src_local * rcv_local * samples,
            4 * traces.size + 4 * start * src_local * LANES,
        ),
        name="transform",
    )(freqs.reshape(-1, 1), traces, *after)


def merge_kernel(core_ref, own_ref, other_ref, *refs):
    blocks = own_ref.shape[1]
    out_refs = refs[-1:] if len(refs[-1].shape) == 6 else refs[-blocks:]
    width = LANES // 2
    is_left = lax.broadcasted_iota(jnp.int32, (1, LANES), 1) < width
    is_first = core_ref[0] == 0
    for block in range(blocks):
        out_ref = out_refs[0].at[0, block] if len(out_refs) == 1 else out_refs[block].at[0]
        for item in range(own_ref.shape[2]):
            own, other = own_ref[0, block, item], other_ref[0, block, item]
            left = jnp.where(is_first, own, other)
            right = jnp.where(is_first, other, own)
            out_ref[item, 0] = jnp.where(is_left, left, pltpu.roll(right, width, 1))
            out_ref[item, 1] = jnp.where(is_left, pltpu.roll(left, width, 1), right)


def merge(core, own, other, start, count, by_src, after=()):
    n_src, n_z, _, rows, _ = own.shape
    spec = pl.BlockSpec((1, n_z, count, rows, LANES), lambda i, c: (i, 0, start // count, 0, 0))
    if by_src:
        out_specs = [pl.BlockSpec((1, n_z, count, 2, rows, LANES), lambda i, c: (i, 0, 0, 0, 0, 0))]
        out_shape = [jax.ShapeDtypeStruct((n_src, n_z, count, 2, rows, LANES), F32)]
    else:
        out_specs = [pl.BlockSpec((1, count, 2, rows, LANES), lambda i, c: (i, 0, 0, 0, 0))] * n_z
        out_shape = [jax.ShapeDtypeStruct((n_src, count, 2, rows, LANES), F32)] * n_z
    return pl.pallas_call(
        merge_kernel,
        grid_spec=pltpu.PrefetchScalarGridSpec(
            num_scalar_prefetch=1,
            grid=(n_src,),
            in_specs=[spec, spec] + [pl.BlockSpec(memory_space=pl.ANY)] * len(after),
            out_specs=out_specs,
        ),
        out_shape=out_shape,
        compiler_params=params(SMALL_VMEM_BYTES),
        cost_estimate=cost(0, 4 * 4 * n_src * n_z * count * rows * LANES),
        name="merge",
    )(core, own, other, *after)


def regroup_kernel(*refs):
    out_ref = refs[-1]
    blocks = out_ref.shape[1]
    for b in range(blocks):
        start = 0
        for ref in (refs[b], refs[blocks + b]):
            stop = start + ref.shape[1]
            out_ref[0, b, start:stop] = ref[0]
            start = stop


def regroup(part, other):
    n_src, _, *rest = part[0].shape
    count = part[0].shape[1] + other[0].shape[1]
    spec = lambda x: pl.BlockSpec((1,) + x.shape[1:], lambda i: (i, 0, 0, 0, 0))
    return pl.pallas_call(
        regroup_kernel,
        grid=(n_src,),
        in_specs=[spec(x) for x in (*part, *other)],
        out_specs=pl.BlockSpec((1, len(part), count, *rest), lambda i: (i, 0, 0, 0, 0, 0)),
        out_shape=jax.ShapeDtypeStruct((n_src, len(part), count, *rest), F32),
        compiler_params=params(SMALL_VMEM_BYTES),
        cost_estimate=cost(0, 8 * len(part) * (part[0].size + other[0].size)),
        name="regroup",
    )(*part, *other)


def beside_kernel(place_ref, block_ref, out_ref):
    out_ref[...] = block_ref[0, :, :, 0]


def beside(place, blocks):
    _, n_z, count, _, size, _ = blocks.shape
    return pl.pallas_call(
        beside_kernel,
        grid_spec=pltpu.PrefetchScalarGridSpec(
            num_scalar_prefetch=1,
            grid=(1,),
            in_specs=[
                pl.BlockSpec(
                    (1, n_z // 2, count, 1, size, size),
                    lambda i, s: (jnp.bitwise_xor(s[1], 1), 1, 0, 1 - s[1] % 2, 0, 0),
                )
            ],
            out_specs=pl.BlockSpec((n_z // 2, count, size, size), lambda i, s: (0, 0, 0, 0)),
        ),
        out_shape=jax.ShapeDtypeStruct((n_z // 2, count, size, size), F32),
        compiler_params=params(SMALL_VMEM_BYTES),
        cost_estimate=cost(0, 4 * n_z * count * size * size),
        name="beside",
    )(place, blocks)


def put_diagonal(out_ref, start, re, im):
    size = re.shape[0]
    row = lax.broadcasted_iota(jnp.int32, (size, size), 0)
    col = lax.broadcasted_iota(jnp.int32, (size, size), 1)
    lower, upper = re + re.T, im + im.T
    both = jnp.where(row > col, lower, jnp.where(row < col, upper, re))
    out_ref[0, start : start + size, :] = both
    diagonal = jnp.sum(jnp.where(row == col, im, 0.0), axis=0, keepdims=True)
    out_ref[0, start + size :, :] = jnp.broadcast_to(diagonal, (8, size))


def pack_kernel(place_ref, block_ref, near_ref, *far_refs):
    size = LANES
    z = place_ref[1]
    for k in range(1, 4):
        for part in range(2):
            start = (2 * (k - 1) + part) * size
            near_ref[0, start : start + size, :] = block_ref[jnp.bitwise_xor(z, k), 1, 0, part]
    put_diagonal(near_ref, 6 * size, block_ref[z, 1, 0, 0], block_ref[z, 1, 0, 1])
    other_half = 2 * (1 - z // 2)
    for far, far_ref in enumerate(far_refs):
        for part in range(2):
            for k in range(2):
                start = (2 * part + k) * size
                far_ref[0, start : start + size, :] = block_ref[other_half + k, 2 + far, 0, part]
        put_diagonal(far_ref, 5 * size, block_ref[z, 2 + far, 0, 0], block_ref[z, 2 + far, 0, 1])


def pack(place, blocks, start, count):
    n_src, n_z, _, _, size, _ = blocks.shape
    near, far = 7 * size + 8, 6 * size + 8
    return pl.pallas_call(
        pack_kernel,
        grid_spec=pltpu.PrefetchScalarGridSpec(
            num_scalar_prefetch=1,
            grid=(count,),
            in_specs=[pl.BlockSpec((n_src, n_z, 1, 2, size, size), lambda j, s: (0, 0, start + j, 0, 0, 0))],
            out_specs=[pl.BlockSpec((1, rows, size), lambda j, s: (j, 0, 0)) for rows in (near, far, far)],
        ),
        out_shape=[jax.ShapeDtypeStruct((count, rows, size), F32) for rows in (near, far, far)],
        compiler_params=params(SMALL_VMEM_BYTES),
        cost_estimate=cost(0, 4 * 2 * blocks.size),
        name="pack",
    )(place, blocks)


def add_beside_kernel(place_ref, block_ref, swapped_ref, *refs):
    for far, far_ref in enumerate(refs[-2:]):
        for j in range(far_ref.shape[0]):
            far_ref[j] = block_ref[0, far, j, 0] + swapped_ref[1 - far, j].T


def add_beside(place, blocks, swapped, packed, start):
    size = LANES
    near, *fars = packed
    count = fars[0].shape[0]
    spec = pl.BlockSpec((count, size, size), lambda i, s: (0, 4, 0))
    anywhere = pl.BlockSpec(memory_space=pl.ANY)
    fars = pl.pallas_call(
        add_beside_kernel,
        grid_spec=pltpu.PrefetchScalarGridSpec(
            num_scalar_prefetch=1,
            grid=(1,),
            in_specs=[
                pl.BlockSpec(
                    (1, 2, count, 1, size, size),
                    lambda i, s: (jnp.bitwise_xor(s[1], 1), 1, start // count, s[1] % 2, 0, 0),
                ),
                pl.BlockSpec((2, count, size, size), lambda i, s: (0, start // count, 0, 0)),
                anywhere,
                anywhere,
            ],
            out_specs=[spec, spec],
        ),
        out_shape=[jax.ShapeDtypeStruct(x.shape, F32) for x in fars],
        input_output_aliases={3: 0, 4: 1},
        compiler_params=params(SMALL_VMEM_BYTES),
        cost_estimate=cost(0, 4 * 6 * count * size * size),
        name="add_beside",
    )(place, blocks, swapped, *fars)
    return [near, *fars]


def take_diagonal(u_ref, there, packed_ref, start):
    size = LANES
    row = lax.broadcasted_iota(jnp.int32, (size, size), 0)
    col = lax.broadcasted_iota(jnp.int32, (size, size), 1)
    at = pl.ds(pl.multiple_of(there * size, size), size)
    both = packed_ref[0, start : start + size, :]
    diagonal = packed_ref[0, start + size : start + size + 1, :]
    u_ref[0, there, at, :] = jnp.where(row >= col, both, 0.0)
    u_ref[1, there, at, :] = jnp.where(row < col, both, jnp.where(row == col, diagonal, 0.0))


def place_packed(u_ref, place_ref, own_ref, near_ref, *far_refs):
    size = LANES
    z = place_ref[1]
    for part in range(2):
        for source in range(4):
            u_ref[part, z, source * size : (source + 1) * size, :] = own_ref[source, 0, 0, part]
    there = jnp.bitwise_xor(z, 1)
    for k in range(1, 4):
        at = pl.ds(pl.multiple_of(jnp.bitwise_xor(there, k) * size, size), size)
        for part in range(2):
            start = (2 * (k - 1) + part) * size
            u_ref[part, there, at, :] = near_ref[0, start : start + size, :]
    take_diagonal(u_ref, there, near_ref, 6 * size)
    half = pl.ds(pl.multiple_of((z // 2) * 2 * size, size), 2 * size)
    for far, far_ref in enumerate(far_refs):
        there = jnp.bitwise_xor(z, 2 + far)
        for part in range(2):
            u_ref[part, there, half, :] = far_ref[0, 2 * part * size : 2 * (part + 1) * size, :]
        at = pl.ds(pl.multiple_of(jnp.bitwise_xor(there, 1) * size, size), size)
        summed = far_ref[0, 4 * size : 5 * size, :]
        is_re = there % 2 == 0
        u_ref[0, there, at, :] = jnp.where(is_re, summed, 0.0)
        u_ref[1, there, at, :] = jnp.where(is_re, 0.0, summed)
        take_diagonal(u_ref, there, far_ref, 5 * size)


def solve_one(u_ref, data_ref, weight, primaries_ref, resid_ref, pred_ref, sums_ref, is_first, before_ref):
    size = LANES
    blocks = u_ref.shape[1]
    for part in range(2):
        for i in range(blocks):
            for k in range(i, blocks):
                here = slice(i * size, (i + 1) * size)
                there = slice(k * size, (k + 1) * size)
                block = 0.5 * (u_ref[part, k, here, :] + u_ref[part, i, there, :].T)
                data_ref[part, here, there] = block
                if k > i:
                    data_ref[part, there, here] = block.T
    data_re, data_im = data_ref[0], data_ref[1]
    re, im, both = halves(data_re), halves(data_im), halves(data_re + data_im)
    prim_re, prim_im = primaries_ref[0, 0], primaries_ref[0, 1]
    first = product(halves(prim_re), re)
    second = product(halves(prim_im), im)
    third = product(halves(prim_re + prim_im), both)
    resid_re = data_re - (first - second)
    resid_im = data_im - (third - first - second)
    resid_ref[0, 0] = resid_re
    resid_ref[0, 1] = resid_im
    cross = product(re, im)
    turned = cross.T
    gram_re = product(both, both) - (cross + turned)
    gram_im = cross - turned
    first = product(halves(resid_re), halves(gram_re))
    second = product(halves(resid_im), halves(gram_im))
    third = product(halves(resid_re + resid_im), halves(gram_re + gram_im))
    pred_re = first - second
    pred_im = third - first - second
    pred_ref[0, 0] = pred_re
    pred_ref[0, 1] = pred_im

    def fold(x):
        x = x.reshape(x.shape[0] // 8, 8, x.shape[1]).sum(0)
        return sum(x[:, k * LANES : (k + 1) * LANES] for k in range(x.shape[1] // LANES))

    numer = weight * fold(resid_re * pred_re + resid_im * pred_im)
    denom = weight * fold(pred_re * pred_re + pred_im * pred_im)

    @pl.when(is_first)
    def _():
        sums_ref[...] = jnp.zeros_like(sums_ref) if before_ref is None else before_ref[...]

    sums_ref[0] += numer
    sums_ref[1] += denom


def place_raw(u_ref, place_ref, block_ref):
    size = LANES
    z = place_ref[1]
    for source in range(block_ref.shape[0]):
        for b in range(block_ref.shape[1]):
            for part in range(2):
                rows = slice(source * size, (source + 1) * size)
                u_ref[part, jnp.bitwise_xor(z, b), rows, :] = block_ref[source, b, 0, part]


def solve_kernel(offset, n_arrived, n_before, place_ref, weight_ref, primaries_ref, *refs):
    before_ref = refs[n_arrived + 2] if n_before else None
    resid_ref, pred_ref, sums_ref, u_ref, data_ref = refs[-5:]
    j = pl.program_id(0)
    if n_arrived == 1:
        place_raw(u_ref, place_ref, refs[0])
    else:
        place_packed(u_ref, place_ref, *refs[:n_arrived])
    solve_one(u_ref, data_ref, weight_ref[offset + j], primaries_ref, resid_ref, pred_ref, sums_ref, j == 0, before_ref)


def solve(place, weights, primaries, arrived, offset, before, start=0):
    size = LANES
    _, _, n, m = primaries.shape
    n_src, n_z = arrived[0].shape[:2]
    count = arrived[-1].shape[2 if len(arrived) == 1 else 0]
    freq = pl.BlockSpec((1, 2, n, m), lambda j, s: (offset + j, 0, 0, 0))
    if len(arrived) == 1:
        specs = [pl.BlockSpec((n_src, n_z, 1, 2, size, size), lambda j, s: (0, 0, j, 0, 0, 0))]
    else:
        specs = [pl.BlockSpec((n_src, 1, 1, 2, size, size), lambda j, s: (0, 0, start + j, 0, 0, 0))]
        for x in arrived[1:]:
            base = start if x.shape[0] > count else 0
            specs.append(pl.BlockSpec((1,) + x.shape[1:], lambda j, s, base=base: (base + j, 0, 0)))
    sums = pl.BlockSpec((2, 8, LANES), lambda j, s: (0, 0, 0))
    n_before = len(before)
    anywhere = pl.BlockSpec(memory_space=pl.ANY)
    at = 3 + len(specs)
    return pl.pallas_call(
        functools.partial(solve_kernel, offset, len(specs), n_before),
        grid_spec=pltpu.PrefetchScalarGridSpec(
            num_scalar_prefetch=1,
            grid=(count,),
            in_specs=[pl.BlockSpec(memory_space=pltpu.SMEM), freq]
            + specs
            + ([anywhere, anywhere, sums] if n_before else []),
            out_specs=[freq, freq, sums],
            scratch_shapes=[
                pltpu.VMEM((2, n // size, n, size), F32),
                pltpu.VMEM((2, n, m), F32),
            ],
        ),
        out_shape=[
            jax.ShapeDtypeStruct(primaries.shape, F32),
            jax.ShapeDtypeStruct(primaries.shape, F32),
            jax.ShapeDtypeStruct((2, 8, LANES), F32),
        ],
        input_output_aliases={at: 0, at + 1: 1} if n_before else {},
        compiler_params=params(),
        cost_estimate=cost(count * 24 * 2 * n * n * m, count * 4 * 2 * n * m * 4),
        name="solve",
    )(place, weights, primaries, *arrived, *before)


def update_kernel(sums_ref, resid_ref, pred_ref, out_ref):
    total = jnp.sum(sums_ref[...], axis=0)
    step = jnp.sum(total[0], keepdims=True) / jnp.sum(total[1], keepdims=True)
    out_ref[...] = resid_ref[...] - step[None, None] * pred_ref[...]


def update(sums, resid, pred):
    count, _, n, m = resid.shape
    rows = pl.BlockSpec((1, 2, n, m), lambda i: (i, 0, 0, 0))
    return pl.pallas_call(
        update_kernel,
        grid=(count,),
        in_specs=[pl.BlockSpec(sums.shape, lambda i: (0, 0, 0, 0)), rows, rows],
        out_specs=rows,
        out_shape=jax.ShapeDtypeStruct(resid.shape, F32),
        compiler_params=params(),
        cost_estimate=cost(2 * resid.size, 12 * resid.size),
        name="update",
    )(sums, resid, pred)


def by_offset(values, n_src, n_rcv):
    bits = n_rcv.bit_length() - 1
    rcv = lax.axis_index("rcv")
    values = values.reshape((n_src,) + (2,) * bits + (-1,))
    for axis in range(bits):
        bit = (rcv >> (bits - 1 - axis)) & 1
        values = jnp.where(bit == 1, jnp.flip(values, axis + 1), values)
    return values.reshape(n_src, n_rcv // 2, 2, -1)


def fence(*arrays):
    return lax.optimization_barrier(arrays)


def chunks_of(freq_local):
    edges = [k * freq_local // 4 for k in range(5)]
    return list(zip(edges[:-1], edges[1:]))


def paired_step(traces, freq_index, primaries):
    src_local, rcv_local, samples = traces.shape
    n_src, n_rcv = lax.axis_size("src"), lax.axis_size("rcv")
    n_z = n_rcv // 2
    freq_local = primaries.shape[0]
    src, rcv = lax.axis_index("src"), lax.axis_index("rcv")
    z, core = rcv // 2, rcv % 2
    place = jnp.stack([src, z]).astype(jnp.int32)
    core_id = core.reshape(1).astype(jnp.int32)

    def along(x, offset):
        return lax.ppermute(x, "rcv", [(i, i ^ offset) for i in range(n_rcv)])

    def along_src(x):
        return lax.all_to_all(x, "src", split_axis=0, concat_axis=0, tiled=True)

    def along_z(blocks):
        return [blocks[0]] + [along(blocks[b], 2 * b) for b in range(1, n_z)]

    chunks = chunks_of(freq_local)
    freqs = by_offset(freq_index, n_src, n_rcv)
    freqs = jnp.transpose(freqs, (2, 0, 1, 3))

    def transformed(groups, after=(), swap=True):
        rows = jnp.concatenate([freqs[..., a:b].reshape(-1) for a, b in groups])
        sizes = [n_src * n_z * (b - a) for a, b in groups for _ in range(2)]
        outs = transform(rows, traces, sizes, after)
        outs = [x.reshape(n_src, n_z, -1, src_local, LANES) for x in outs]
        pairs = [(outs[2 * i], outs[2 * i + 1]) for i in range(len(groups))]
        return [(own, along(away, 1) if swap else away) for own, away in pairs]

    weights = freq_index.astype(jnp.float32) / (samples // 2)
    weights = lax.dynamic_slice_in_dim(weights, (src * n_rcv + rcv) * freq_local, freq_local)

    a, b, c, d = chunks
    size = [stop - start for start, stop in chunks]
    a1, a2 = (a[0], a[0] + size[0] // 2), (a[0] + size[0] // 2, a[1])
    half_d = size[3] // 2
    spec_a1, spec_b, spec_a2, spec_c = transformed([a1, b, a2, c])
    first_a1 = merge(core_id, *spec_a1, 0, a1[1] - a1[0], False)
    sent_b = merge(core_id, *spec_b, 0, size[1], True, (first_a1[0],))[0]
    *first_a1, sent_b = fence(*first_a1, sent_b)

    raw_a1 = along_z(first_a1)
    arrived_b = along_src(sent_b)
    first_a2 = merge(core_id, *spec_a2, 0, a2[1] - a2[0], False, (sent_b,))
    sent_c = merge(core_id, *spec_c, 0, size[2], True, (sent_b,))[0]
    (spec_d,) = transformed([d], (sent_b,), False)
    *all_a, arrived_b, sent_c, own_d, away_d, p, q, r, t = fence(
        *raw_a1, arrived_b, sent_c, *spec_d, *first_a2
    )

    raw_a2 = along_z([p, q, r, t])
    arrived_c = along_src(sent_c)
    swapped = along(beside(place, arrived_b), 2)
    packed = pack(place, arrived_b, 0, size[1])
    sent_d = merge(core_id, own_d, along(away_d, 1), 0, size[3], True)[0]
    *all_a, arrived_b, arrived_c, sent_d, swapped, p, q, r = fence(
        *all_a, *raw_a2, arrived_b, arrived_c, sent_d, swapped, *packed
    )

    here_b = along_z([arrived_b] + add_beside(place, arrived_b, swapped, (p, q, r), 0))
    arrived_d = along_src(sent_d)
    swapped = along(beside(place, arrived_c), 2)
    packed = pack(place, arrived_c, 0, size[2])
    whole_a = regroup(all_a[:n_z], all_a[n_z:])
    *here_b, arrived_c, arrived_d, whole_a, swapped, p, q, r = fence(
        *here_b, arrived_c, arrived_d, whole_a, swapped, *packed
    )

    here_c = along_z([arrived_c] + add_beside(place, arrived_c, swapped, (p, q, r), 0))
    whole_a = along_src(whole_a)
    swapped = along(beside(place, arrived_d), 2)
    near = pack(place, arrived_d, 0, size[3])[0]
    far_1 = pack(place, arrived_d, 0, half_d)[1:]
    far_2 = pack(place, arrived_d, half_d, size[3] - half_d)[1:]
    packed = [near, *far_1, *far_2]
    before = solve(place, weights, primaries, here_b, b[0], ())
    *here_c, arrived_d, whole_a, swapped, p, q, r, t, u, x, y, w = fence(
        *here_c, arrived_d, whole_a, swapped, *packed, *before
    )

    here_d = along_z([arrived_d] + add_beside(place, arrived_d, swapped, (p, q, r), 0))
    _, *fars = add_beside(place, arrived_d, swapped, (p, t, u), half_d)
    last_d = here_d[:2] + [along(x, 2 * b) for b, x in enumerate(fars, 2)]
    before = solve(place, weights, primaries, [whole_a], a[0], (x, y, w))
    before = solve(place, weights, primaries, here_c, c[0], before)
    before = solve(place, weights, primaries, here_d, d[0], before)
    before = solve(place, weights, primaries, last_d, d[0] + half_d, before, half_d)

    resid, pred, sums = before
    sums = jnp.broadcast_to(sums[None], (n_src * n_rcv,) + sums.shape)
    sums = lax.all_to_all(sums, AXES, split_axis=0, concat_axis=0, tiled=True)
    return (resid, update(sums, resid, pred))


def solution(mesh):
    in_specs = (P("src", "rcv", None), P(), P(("src", "rcv"), None, None, None))
    out_specs = (P(("src", "rcv"), None, None, None), P(("src", "rcv"), None, None, None))
    n_src, n_rcv = mesh.shape["src"], mesh.shape["rcv"]

    def step(traces, freq_index, primaries):
        src_local, rcv_local, _ = traces.shape
        square = src_local == LANES and 2 * rcv_local == LANES
        if square and n_src == 4 and n_rcv == 2 * n_src and primaries.shape[0] >= 8:
            return paired_step(traces, freq_index, primaries)
        return plain_step(traces, freq_index, primaries)

    return jax.shard_map(step, mesh=mesh, in_specs=in_specs, out_specs=out_specs, check_vma=False)
```
